32 devices in a mesh: seg: 8 (over z, y), row: 4 (over x, core).
Axes of the slice: x: 2, y: 2, z: 4, core: 2. Of those that a mesh axis runs over, the one named last changes fastest.
Arguments:
- left_env: float32 [8, 128, 6, 2048], P('seg', None, None, 'row'), may hold values from -4 to 4
- left_core: float32 [8, 2048, 2, 2048], P('seg', None, None, 'row'), may hold values from -0.125 to 0.125
- inv_sing: float32 [8, 2048], P('seg', 'row'), may hold values from 1 to 8
- mpo_pair: float32 [8, 2, 6, 6, 2, 2], P('seg'), may hold values from -1.75 to 1.75
- right_core: float32 [8, 2048, 2, 2048], P('seg', None, None, 'row'), may hold values from -0.125 to 0.125
- right_env: float32 [8, 6, 2048, 2048], P('seg', None, 'row'), may hold values from -0.078125 to 0.078125
Outputs:
- applied: float32 [8, 128, 2, 2, 2048], P('seg', None, None, None, 'row')
The draws below stay inside these ranges and needn't reach their ends.
All inputs are finite; a program needn't handle non-finite values.
Results may differ from the reference program's by a relative error of at most 0.0003.
Values sent between devices are 32-bit elements; how exact they have to be, the bound alone decides.
No kernel may reach another device: no remote copies, remote signals or barrier semaphores. Data moves between devices by JAX's collectives and lax.ppermute only.
A program may use at most 192 MiB of HBM per device.

```python
import math
import jax
import jax.numpy as jnp
from jax import lax

CHI = 2048
W = 6
P_SIZE = 128
NSEG = 8


def raised(values, key, source, target, parts, factor):
    owner, partner = [(jnp.arange(values.shape[position]) // (values.shape[position] // parts)).reshape([-1 if axis == position else 1 for axis in range(values.ndim)]) for position in (source, target)]
    chosen = jax.random.permutation(key, parts)[partner]
    strong = (owner == chosen) | (owner == (partner + parts // 2) % parts)
    return jnp.where(strong, factor * values, values)


def steps_of(key, dims, pieces, least, largest):
    loudness = 1.0
    for axis_at, parts in pieces:
        heights = jax.random.uniform(jax.random.fold_in(jax.random.fold_in(key, 6), axis_at), (parts,), jnp.float32, least / len(pieces), largest / len(pieces))
        loudness = loudness * jnp.repeat(jnp.exp(heights), dims[axis_at] // parts).reshape((-1,) + (1,) * (len(dims) - 1 - axis_at))
    return loudness


def bell_draw(own_key, shape, deviation, bound, pieces=(), held_as=jnp.bfloat16):
    values = deviation * jax.random.normal(own_key, shape, jnp.float32)
    if pieces:
        values = values * steps_of(own_key, shape, pieces, -0.22, 0.18)
    return jnp.clip(values, -bound, bound).astype(held_as)


def noise_with(rng, extent, spread, most, cuts, heavy, kind=jnp.bfloat16):
    array = spread * jax.random.normal(rng, extent, jnp.float32)
    if cuts:
        array = array * steps_of(rng, extent, cuts, -0.22, 0.18)
    return jnp.clip(raised(array, jax.random.fold_in(rng, 3), *heavy), -most, most).astype(kind)


def setup_inputs(seed: int = 0) -> dict:
    key_of = jax.random.split(jax.random.key(seed), 7)
    return {
        "left_env": bell_draw(key_of[0], (NSEG, P_SIZE, W, CHI), 0.25, 4.0, ((0, 8), (3, 4)), jnp.float32),
        "left_core": bell_draw(key_of[1], (NSEG, CHI, 2, CHI), CHI ** -0.5, 0.125, ((0, 8), (3, 4)), jnp.float32),
        "inv_sing": jnp.clip(jnp.exp(math.log(8.0) - 2.0794415 * jax.random.uniform(key_of[2], (NSEG, CHI), jnp.float32) ** steps_of(key_of[2], (NSEG, CHI), ((0, 8), (1, 4)), -0.2, 0.2)), 1.0, 8.0),
        "mpo_pair": bell_draw(key_of[3], (NSEG, 2, W, W, 2, 2), (2 * W) ** -0.5, 1.75, ((0, 8),), jnp.float32),
        "right_core": bell_draw(key_of[4], (NSEG, CHI, 2, CHI), CHI ** -0.5, 0.125, ((0, 8), (3, 4)), jnp.float32),
        "right_env": noise_with(key_of[5], (NSEG, W, CHI, CHI), (W * CHI) ** -0.5, 0.078125, ((0, 8), (2, 4)), (2, 3, 4, 2.0), jnp.float32),
    }


def one_boundary(index, left_env, left_core, inv_sing, mpo_pair, right_core, right_env):
    high = lax.Precision.HIGHEST
    nxt = jnp.minimum(index + 1, NSEG - 1).astype(jnp.int32)
    env_l = lax.dynamic_index_in_dim(left_env, index, 0, keepdims=False)
    core_l = lax.dynamic_index_in_dim(left_core, index, 0, keepdims=False)
    scales = lax.dynamic_index_in_dim(inv_sing, index, 0, keepdims=False)
    pair = lax.dynamic_index_in_dim(mpo_pair, index, 0, keepdims=False)
    core_r = lax.dynamic_index_in_dim(right_core, nxt, 0, keepdims=False)
    env_r = lax.dynamic_index_in_dim(right_env, nxt, 0, keepdims=False)
    lefted = jnp.dot(env_l.reshape(P_SIZE * W, CHI), core_l.reshape(CHI, 2 * CHI), precision=high, preferred_element_type=jnp.float32)
    scaled = lefted.reshape(P_SIZE, W, 2, CHI) * scales
    paired = jnp.dot(scaled.reshape(P_SIZE * W * 2, CHI), core_r.reshape(CHI, 2 * CHI), precision=high, preferred_element_type=jnp.float32)
    paired = paired.reshape(P_SIZE, W, 2, 2, CHI)
    first = jnp.einsum('xyps,axstc->apytc', pair[0], paired, precision=high)
    mixed = jnp.einsum('yzqt,apytc->apqzc', pair[1], first, precision=high)
    result = jnp.dot(mixed.reshape(P_SIZE * 4, W * CHI), env_r.reshape(W * CHI, CHI), precision=high, preferred_element_type=jnp.float32)
    live = (index < NSEG - 1).astype(jnp.float32)
    return result.reshape(P_SIZE, 2, 2, CHI) * live


def reference(left_env, left_core, inv_sing, mpo_pair, right_core, right_env):
    indices = jnp.arange(NSEG, dtype=jnp.int32)
    return lax.map(lambda index: one_boundary(index, left_env, left_core, inv_sing, mpo_pair, right_core, right_env), indices)
```

```python
import functools

import jax
import jax.numpy as jnp
from jax import lax
from jax.experimental import pallas as pl
from jax.experimental.pallas import tpu as pltpu
from jax.sharding import PartitionSpec as P

MIB = 1024 * 1024
CHUNKS = 4


def shifted(value, axis, steps):
    count = lax.axis_size(axis)
    first, last = (max(0, -steps), min(count, count - steps))
    return lax.ppermute(value, axis, [(source, source + steps) for source in range(first, last)])


def swapped(value, axis, bit):
    count = lax.axis_size(axis)
    return lax.ppermute(value, axis, [(source, source ^ bit) for source in range(count)])


def gathered(own, axis):
    bit = lax.axis_size(axis) // 2
    pieces = {0: own}
    while bit:
        for d in list(pieces):
            pieces[d ^ bit] = swapped(pieces[d], axis, bit)
        bit //= 2
    return [pieces[d] for d in range(len(pieces))]


def halves(x):
    hi = x.astype(jnp.bfloat16)
    lo = (x - hi.astype(jnp.float32)).astype(jnp.bfloat16)
    return hi, lo


def product(hi, lo, w_hi, w_lo):
    rows = hi.shape[0]
    both = jnp.dot(jnp.concatenate([hi, lo], 0), w_hi, preferred_element_type=jnp.float32)
    return both[:rows] + both[rows:] + jnp.dot(hi, w_lo, preferred_element_type=jnp.float32)


def split_core_kernel(x_ref, hi_ref, lo_ref):
    for i in range(x_ref.shape[1]):
        hi, lo = halves(x_ref[:, i, :])
        hi_ref[i] = hi
        lo_ref[i] = lo


def split_core(core):
    bond, spins, cols = core.shape
    block = 256
    out = jax.ShapeDtypeStruct((spins, bond, cols), jnp.bfloat16)
    spec = pl.BlockSpec((spins, block, cols), lambda t: (0, t, 0))
    return pl.pallas_call(
        split_core_kernel,
        grid=(bond // block,),
        in_specs=[pl.BlockSpec((block, spins, cols), lambda t: (t, 0, 0))],
        out_specs=[spec, spec],
        out_shape=[out, out],
        compiler_params=pltpu.CompilerParams(vmem_limit_bytes=16 * MIB),
        cost_estimate=pl.CostEstimate(
            flops=4 * core.size, bytes_accessed=8 * core.size, transcendentals=0
        ),
        name="split_core",
    )(core)


def split_env_kernel(x_ref, hi_ref, lo_ref):
    hi_ref[...], lo_ref[...] = halves(x_ref[...])


def split_env(env):
    rows, cols = env.shape
    block = 256
    out = jax.ShapeDtypeStruct((rows, cols), jnp.bfloat16)
    spec = pl.BlockSpec((block, cols), lambda t: (t, 0))
    return pl.pallas_call(
        split_env_kernel,
        grid=(rows // block,),
        in_specs=[spec],
        out_specs=[spec, spec],
        out_shape=[out, out],
        compiler_params=pltpu.CompilerParams(vmem_limit_bytes=16 * MIB),
        cost_estimate=pl.CostEstimate(
            flops=4 * env.size, bytes_accessed=8 * env.size, transcendentals=0
        ),
        name="split_env",
    )(env)


def left_kernel(count, row_ref, mpo_ref, *refs):
    pieces = refs[:count]
    hi_ref, lo_ref, inv_ref, out_ref, acc_ref = refs[count:]
    i = pl.program_id(0)
    width, panel, cols = pieces[0].shape
    for d in range(count):
        hi, lo = halves(pieces[d][...].reshape(width * panel, cols))
        rows = pl.ds(pl.multiple_of((row_ref[0] ^ d) * cols, cols), cols)
        term = product(hi, lo, hi_ref[0, rows, :], lo_ref[0, rows, :])
        if d == 0:
            acc_ref[...] = term
        else:
            acc_ref[...] += term
    inv = inv_ref[...]

    def mix(add):
        for p in range(2):
            for y in range(width):
                total = None
                for w in range(width):
                    scalar = mpo_ref[((w * width + y) * 2 + p) * 2 + i]
                    value = scalar * acc_ref[w * panel:(w + 1) * panel, :]
                    total = value if total is None else total + value
                total = total * inv
                if add:
                    total = total + out_ref[p * width + y]
                out_ref[p * width + y] = total

    pl.when(i == 0)(lambda: mix(False))
    pl.when(i != 0)(lambda: mix(True))


def left_block(row, mpo, pieces, core_hi, core_lo, inv):
    width, panel, cols = pieces[0].shape
    spins, bond, _ = core_hi.shape
    count = len(pieces)
    piece_spec = pl.BlockSpec((width, panel, cols), lambda i, row: (0, 0, 0))
    core_spec = pl.BlockSpec((1, bond, cols), lambda i, row: (i, 0, 0))
    macs = width * panel * bond * spins * cols
    return pl.pallas_call(
        functools.partial(left_kernel, count),
        grid_spec=pltpu.PrefetchScalarGridSpec(
            num_scalar_prefetch=1,
            grid=(spins,),
            in_specs=[pl.BlockSpec(memory_space=pltpu.SMEM)]
            + [piece_spec] * count
            + [core_spec, core_spec, pl.BlockSpec((1, cols), lambda i, row: (0, 0))],
            out_specs=pl.BlockSpec((2 * width, panel, cols), lambda i, row: (0, 0, 0)),
            scratch_shapes=[pltpu.VMEM((width * panel, cols), jnp.float32)],
        ),
        out_shape=jax.ShapeDtypeStruct((2 * width, panel, cols), jnp.float32),
        compiler_params=pltpu.CompilerParams(vmem_limit_bytes=32 * MIB),
        cost_estimate=pl.CostEstimate(
            flops=6 * macs, bytes_accessed=4 * core_hi.size, transcendentals=0
        ),
        name="left_block",
    )(row, mpo, *pieces, core_hi, core_lo, inv)


def right_kernel(count, row_ref, mpo_ref, *refs):
    pieces = refs[:count]
    core_hi, core_lo, env_hi, env_lo, send_ref, keep_ref, first_ref, mh_ref, ml_ref = refs[count:]
    t = pl.program_id(0)
    blocks, panel, cols = pieces[0].shape
    width = blocks // 2

    def pair():
        for d in range(count):
            hi, lo = halves(pieces[d][...].reshape(blocks * panel, cols))
            rows = pl.ds(pl.multiple_of((row_ref[0] ^ d) * cols, cols), cols)
            term = product(hi, lo, core_hi[0, rows, :], core_lo[0, rows, :])
            if d == 0:
                first_ref[t] = term
            else:
                first_ref[t] += term

    def mix():
        for p in range(2):
            for q in range(2):
                for z in range(width):
                    total = None
                    for y in range(width):
                        for j in range(2):
                            scalar = mpo_ref[((y * width + z) * 2 + q) * 2 + j]
                            start = (p * width + y) * panel
                            value = scalar * first_ref[j, start:start + panel, :]
                            total = value if total is None else total + value
                    hi, lo = halves(total)
                    at = (p * 2 + q) * panel
                    mh_ref[at:at + panel, z * cols:(z + 1) * cols] = hi
                    ml_ref[at:at + panel, z * cols:(z + 1) * cols] = lo

    def close():
        result = product(mh_ref[...], ml_ref[...], env_hi[...], env_lo[...])
        half = count // 2

        @pl.when(t - 2 < half)
        def _():
            send_ref[jnp.minimum(t - 2, half - 1)] = result

        @pl.when(t - 2 >= half)
        def _():
            keep_ref[jnp.maximum(t - 2 - half, 0)] = result

    pl.when(t < 2)(pair)
    pl.when(t == 2)(mix)
    pl.when(t >= 2)(close)


def right_block(row, mpo, pieces, core_hi, core_lo, env_hi, env_lo):
    blocks, panel, cols = pieces[0].shape
    spins, bond, _ = core_hi.shape
    inner, outer = env_hi.shape
    count = len(pieces)
    half = count // 2
    out_cols = outer // count

    def env_at(t, row):
        k = jnp.maximum(t - 2, 0)
        d = jnp.where(k < half, 2 * k + 1, 2 * (k - half))
        return 0, row[0] ^ d

    whole = lambda t, row: (0, 0, 0)
    piece_spec = pl.BlockSpec((blocks, panel, cols), whole)
    core_spec = pl.BlockSpec((1, bond, cols), lambda t, row: (jnp.minimum(t, 1), 0, 0))
    env_spec = pl.BlockSpec((inner, out_cols), env_at)
    out_spec = pl.BlockSpec((half, 4 * panel, out_cols), whole)
    out = jax.ShapeDtypeStruct((half, 4 * panel, out_cols), jnp.float32)
    macs = blocks * panel * bond * spins * cols + 4 * panel * inner * outer
    return pl.pallas_call(
        functools.partial(right_kernel, count),
        grid_spec=pltpu.PrefetchScalarGridSpec(
            num_scalar_prefetch=1,
            grid=(2 + count,),
            in_specs=[pl.BlockSpec(memory_space=pltpu.SMEM)]
            + [piece_spec] * count
            + [core_spec, core_spec, env_spec, env_spec],
            out_specs=[out_spec, out_spec],
            scratch_shapes=[
                pltpu.VMEM((2, blocks * panel, cols), jnp.float32),
                pltpu.VMEM((4 * panel, inner), jnp.bfloat16),
                pltpu.VMEM((4 * panel, inner), jnp.bfloat16),
            ],
        ),
        out_shape=[out, out],
        compiler_params=pltpu.CompilerParams(vmem_limit_bytes=48 * MIB),
        cost_estimate=pl.CostEstimate(
            flops=6 * macs,
            bytes_accessed=4 * (core_hi.size + env_hi.size),
            transcendentals=0,
        ),
        name="right_block",
    )(row, mpo, *pieces, core_hi, core_lo, env_hi, env_lo)


def per_device(left_env, left_core, inv_sing, mpo_pair, right_core, right_env):
    count = lax.axis_size("row")
    row = lax.axis_index("row").astype(jnp.int32).reshape(1)
    panel = left_env.shape[1]
    part = panel // CHUNKS
    cols = left_core.shape[3]
    env = left_env[0].transpose(1, 0, 2)
    mpo_left = mpo_pair[0, 0].reshape(-1)
    mpo_right = shifted(mpo_pair[0, 1].reshape(-1), "seg", 1)
    lc_hi, lc_lo = split_core(left_core[0])
    rc_hi, rc_lo = split_core(right_core[0])
    inner = right_env.shape[1] * right_env.shape[2]
    re_hi, re_lo = split_env(right_env[0].reshape(inner, right_env.shape[3]))
    outs = []
    for k in range(CHUNKS):
        own = lax.slice_in_dim(env, k * part, (k + 1) * part, axis=1)
        pieces = gathered(own, "row")
        scaled = left_block(row, mpo_left, pieces, lc_hi, lc_lo, inv_sing)
        scaled = shifted(scaled, "seg", 1)
        pieces = gathered(scaled, "row")
        send, keep = right_block(row, mpo_right, pieces, rc_hi, rc_lo, re_hi, re_lo)
        came = swapped(send, "row", 1)
        sums = [keep[m] + came[m] for m in range(count // 2)]
        bit = 2
        while len(sums) > 1:
            came = [swapped(value, "row", bit) for value in sums[1::2]]
            sums = [one + two for one, two in zip(sums[0::2], came)]
            bit *= 2
        back = shifted(sums[0], "seg", -1)
        outs.append(back.reshape(2, 2, part, cols).transpose(2, 0, 1, 3))
    return jnp.concatenate(outs, 0)[None]


def solution(mesh):
    return jax.shard_map(
        per_device,
        mesh=mesh,
        in_specs=(
            P("seg", None, None, "row"),
            P("seg", None, None, "row"),
            P("seg", "row"),
            P("seg", None, None, None, None, None),
            P("seg", None, None, "row"),
            P("seg", None, "row", None),
        ),
        out_specs=P("seg", None, None, None, "row"),
        check_vma=False,
    )
```

```python
import functools

import jax
import jax.numpy as jnp
from jax import lax
from jax.experimental import pallas as pl
from jax.experimental.pallas import tpu as pltpu
from jax.sharding import PartitionSpec as P

MIB = 1024 * 1024
LANES = 128
WIDE = 256
SIZES = (32, 32, 32, 32)
FETCHES = (1, 1, 2)

IN_VMEM = pl.BlockSpec(memory_space=pltpu.VMEM)
IN_SMEM = pl.BlockSpec(memory_space=pltpu.SMEM)
ANYWHERE = pl.BlockSpec(memory_space=pl.ANY)


def shifted(value, axis, steps):
    count = lax.axis_size(axis)
    first, last = (max(0, -steps), min(count, count - steps))
    return lax.ppermute(value, axis, [(source, source + steps) for source in range(first, last)])


def swapped(value, axis, bit):
    count = lax.axis_size(axis)
    return lax.ppermute(value, axis, [(source, source ^ bit) for source in range(count)])


def gathered(own, axis):
    bit = lax.axis_size(axis) // 2
    pieces = {0: own}
    while bit:
        for d in list(pieces):
            pieces[d ^ bit] = swapped(pieces[d], axis, bit)
        bit //= 2
    return [pieces[d] for d in range(len(pieces))]


def in_vmem(*values):
    return [pltpu.with_memory_space_constraint(value, pltpu.VMEM) for value in values]


def halves(x):
    hi = x.astype(jnp.bfloat16)
    lo = (x - hi.astype(jnp.float32)).astype(jnp.bfloat16)
    return hi, lo


def product(both, w_hi, w_lo):
    rows = both.shape[0] // 2
    wide = jnp.dot(both, w_hi, preferred_element_type=jnp.float32)
    return wide[:rows] + wide[rows:] + jnp.dot(
        both[:rows], w_lo, preferred_element_type=jnp.float32
    )


def streamed(x_hbm, buffers, sems, body):
    block = buffers.shape[1]
    steps = x_hbm.shape[0] // block

    def copy(t):
        slot = lax.rem(t, 2)
        rows = pl.ds(pl.multiple_of(t * block, block), block)
        return pltpu.make_async_copy(x_hbm.at[rows], buffers.at[slot], sems.at[slot])

    copy(0).start()

    @pl.loop(0, steps)
    def _(t):
        @pl.when(t + 1 < steps)
        def _():
            copy(t + 1).start()

        copy(t).wait()
        body(t, buffers.at[lax.rem(t, 2)])


def split_core_kernel(spins, tiles, x_hbm, hi_ref, lo_ref, buffers, sems):
    step = spins * tiles
    block = buffers.shape[1] // step

    def body(t, x_ref):
        rows = pl.ds(pl.multiple_of(t * block, block), block)
        for tile in range(tiles):
            for i in range(spins):
                x = x_ref[pl.ds(tile * spins + i, block, stride=step), :]
                hi, lo = halves(x)
                lanes = slice(tile * LANES, (tile + 1) * LANES)
                hi_ref[i, rows, lanes] = hi
                lo_ref[i, rows, lanes] = lo

    streamed(x_hbm, buffers, sems, body)


def split_core(core):
    bond, spins, cols = core.shape
    tiles = cols // LANES
    step = spins * tiles
    block = 256
    flat = core.reshape(bond, spins, tiles, LANES).transpose(0, 2, 1, 3).reshape(bond * step, LANES)
    flat = pltpu.with_memory_space_constraint(flat, pltpu.HBM)
    out = pltpu.VMEM((spins, bond, cols), jnp.bfloat16)
    return pl.pallas_call(
        functools.partial(split_core_kernel, spins, tiles),
        in_specs=[ANYWHERE],
        out_specs=[IN_VMEM, IN_VMEM],
        out_shape=[out, out],
        scratch_shapes=[
            pltpu.VMEM((2, block * step, LANES), jnp.float32),
            pltpu.SemaphoreType.DMA((2,)),
        ],
        compiler_params=pltpu.CompilerParams(vmem_limit_bytes=8 * MIB),
        cost_estimate=pl.CostEstimate(
            flops=4 * core.size, bytes_accessed=8 * core.size, transcendentals=0
        ),
        name="split_core",
    )(flat)


def split_env_kernel(x_hbm, hi_ref, lo_ref, buffers, sems):
    block = buffers.shape[1]

    def body(t, x_ref):
        rows = pl.ds(pl.multiple_of(t * block, block), block)
        hi_ref[rows, :], lo_ref[rows, :] = halves(x_ref[...])

    streamed(x_hbm, buffers, sems, body)


def split_env(env):
    rows, cols = env.shape
    block = 128
    env = pltpu.with_memory_space_constraint(env, pltpu.HBM)
    out = pltpu.VMEM((rows, cols), jnp.bfloat16)
    return pl.pallas_call(
        split_env_kernel,
        in_specs=[ANYWHERE],
        out_specs=[IN_VMEM, IN_VMEM],
        out_shape=[out, out],
        scratch_shapes=[
            pltpu.VMEM((2, block, cols), jnp.float32),
            pltpu.SemaphoreType.DMA((2,)),
        ],
        compiler_params=pltpu.CompilerParams(vmem_limit_bytes=8 * MIB),
        cost_estimate=pl.CostEstimate(
            flops=4 * env.size, bytes_accessed=4 * env.size, transcendentals=0
        ),
        name="split_env",
    )(env)


def lay_out(row, pieces, both_ref):
    rows = both_ref.shape[0] // 2
    for d, x in enumerate(pieces):
        cols = x.shape[-1]
        hi, lo = halves(x.reshape(rows, cols))
        at = pl.ds(pl.multiple_of((row ^ d) * cols, cols), cols)
        both_ref[:rows, at] = hi
        both_ref[rows:, at] = lo


def left_kernel(count, starts, panel, row_ref, mpo_ref, *refs):
    pieces = refs[:count]
    hi_ref, lo_ref, inv_ref, out_ref, both_ref, acc_ref = refs[count:]
    width = pieces[0].shape[0]
    spins, _, cols = hi_ref.shape
    wide = min(WIDE, cols)
    lay_out(
        row_ref[0],
        [ref[:, start:start + panel, :] for ref, start in zip(pieces, starts)],
        both_ref,
    )
    for i in range(spins):
        for c in range(0, cols, wide):
            at = slice(c, c + wide)
            acc_ref[i, :, at] = product(both_ref[...], hi_ref[i, :, at], lo_ref[i, :, at])
    for c in range(0, cols, wide):
        at = slice(c, c + wide)
        inv = inv_ref[:, at]
        for p in range(2):
            for y in range(width):
                total = None
                for w in range(width):
                    for i in range(spins):
                        scalar = mpo_ref[((w * width + y) * 2 + p) * 2 + i]
                        value = scalar * acc_ref[i, w * panel:(w + 1) * panel, at]
                        total = value if total is None else total + value
                out_ref[p * width + y, :, at] = total * inv


def left_block(row, mpo, pieces, starts, panel, core_hi, core_lo, inv):
    width, _, cols = pieces[0].shape
    spins, bond, _ = core_hi.shape
    count = len(pieces)
    macs = width * panel * bond * spins * cols
    return pl.pallas_call(
        functools.partial(left_kernel, count, starts, panel),
        in_specs=[IN_SMEM] * 2 + [IN_VMEM] * (count + 3),
        out_specs=IN_VMEM,
        out_shape=jax.ShapeDtypeStruct((2 * width, panel, cols), jnp.float32),
        scratch_shapes=[
            pltpu.VMEM((2 * width * panel, bond), jnp.bfloat16),
            pltpu.VMEM((spins, width * panel, cols), jnp.float32),
        ],
        compiler_params=pltpu.CompilerParams(vmem_limit_bytes=8 * MIB),
        cost_estimate=pl.CostEstimate(
            flops=8 * macs, bytes_accessed=0, transcendentals=0
        ),
        name="left_block",
    )(row, mpo, *pieces, *in_vmem(core_hi, core_lo), inv)


def right_kernel(count, row_ref, mpo_ref, *refs):
    pieces = refs[:count]
    core_hi, core_lo, env_hi, env_lo, send_ref, keep_ref = refs[count:count + 6]
    both_ref, first_ref, mixed_ref = refs[count + 6:]
    row = row_ref[0]
    blocks, panel, cols = pieces[0].shape
    width = blocks // 2
    spins = core_hi.shape[0]
    wide = min(WIDE, cols)
    lay_out(row, [ref[...] for ref in pieces], both_ref)
    for c in range(0, cols, wide):
        at = slice(c, c + wide)
        for j in range(spins):
            first_ref[j, :, at] = product(both_ref[...], core_hi[j, :, at], core_lo[j, :, at])
    for c in range(0, cols, wide):
        at = slice(c, c + wide)
        for p in range(2):
            for q in range(2):
                to = (p * 2 + q) * panel
                for z in range(width):
                    total = None
                    for y in range(width):
                        for j in range(spins):
                            scalar = mpo_ref[((y * width + z) * 2 + q) * 2 + j]
                            start = (p * width + y) * panel
                            value = scalar * first_ref[j, start:start + panel, at]
                            total = value if total is None else total + value
                    hi, lo = halves(total)
                    lanes = slice(z * cols + c, z * cols + c + wide)
                    mixed_ref[to:to + panel, lanes] = hi
                    mixed_ref[4 * panel + to:5 * panel + to, lanes] = lo
    for d in [*range(1, count, 2), *range(0, count, 2)]:
        out_ref = send_ref if d % 2 else keep_ref
        out_cols = out_ref.shape[2]
        wide = min(WIDE, out_cols)
        for c in range(0, out_cols, wide):
            at = pl.ds(pl.multiple_of((row ^ d) * out_cols + c, wide), wide)
            out_ref[d // 2, :, c:c + wide] = product(
                mixed_ref[...], env_hi[:, at], env_lo[:, at]
            )


def right_block(row, mpo, pieces, core_hi, core_lo, env_hi, env_lo):
    blocks, panel, cols = pieces[0].shape
    spins, bond, _ = core_hi.shape
    inner, outer = env_hi.shape
    count = len(pieces)
    out = jax.ShapeDtypeStruct((count // 2, 4 * panel, outer // count), jnp.float32)
    macs = blocks * panel * bond * spins * cols + 4 * panel * inner * outer
    return pl.pallas_call(
        functools.partial(right_kernel, count),
        in_specs=[IN_SMEM] * 2 + [IN_VMEM] * (count + 4),
        out_specs=[IN_VMEM, IN_VMEM],
        out_shape=[out, out],
        scratch_shapes=[
            pltpu.VMEM((2 * blocks * panel, bond), jnp.bfloat16),
            pltpu.VMEM((spins, blocks * panel, cols), jnp.float32),
            pltpu.VMEM((8 * panel, inner), jnp.bfloat16),
        ],
        compiler_params=pltpu.CompilerParams(vmem_limit_bytes=14 * MIB),
        cost_estimate=pl.CostEstimate(
            flops=8 * macs, bytes_accessed=0, transcendentals=0
        ),
        name="right_block",
    )(row, mpo, *pieces, *in_vmem(core_hi, core_lo, env_hi, env_lo))


def per_device(left_env, left_core, inv_sing, mpo_pair, right_core, right_env):
    count = lax.axis_size("row")
    row = lax.axis_index("row").astype(jnp.int32).reshape(1)
    env = left_env[0].transpose(1, 0, 2)
    mpo_left = mpo_pair[0, 0].reshape(-1)
    mpo_right = shifted(mpo_pair[0, 1].reshape(-1), "seg", 1)

    inner = right_env.shape[1] * right_env.shape[2]
    core_a = split_core(left_core[0])
    core_b = split_core(right_core[0])
    env_b = split_env(right_env[0].reshape(inner, right_env.shape[3]))

    fetched = []
    begin = 0
    k = 0
    for number in FETCHES:
        sizes = SIZES[k:k + number]
        k += number
        own = lax.slice_in_dim(env, begin, begin + sum(sizes), axis=1)
        pieces = gathered(own, "row")
        start = 0
        for size in sizes:
            fetched.append((pieces, start, size))
            start += size
        begin += start

    outs = []
    for pieces, start, size in fetched:
        scaled = left_block(row, mpo_left, pieces, [start] * count, size, *core_a, inv_sing)
        pieces = gathered(shifted(scaled, "seg", 1), "row")
        send, keep = right_block(row, mpo_right, pieces, *core_b, *env_b)
        came = swapped(send, "row", 1)
        sums = [keep[m] + came[m] for m in range(count // 2)]
        bit = 2
        while len(sums) > 1:
            came = [swapped(value, "row", bit) for value in sums[1::2]]
            sums = [one + two for one, two in zip(sums[0::2], came)]
            bit *= 2
        back = shifted(sums[0], "seg", -1)
        outs.append(back.reshape(2, 2, size, back.shape[1]).transpose(2, 0, 1, 3))
    return jnp.concatenate(outs, 0)[None]


def solution(mesh):
    return jax.shard_map(
        per_device,
        mesh=mesh,
        in_specs=(
            P("seg", None, None, "row"),
            P("seg", None, None, "row"),
            P("seg", "row"),
            P("seg", None, None, None, None, None),
            P("seg", None, None, "row"),
            P("seg", None, "row", None),
        ),
        out_specs=P("seg", None, None, None, "row"),
        check_vma=False,
    )
```

```python
import functools

import jax
import jax.numpy as jnp
from jax import lax
from jax.experimental import pallas as pl
from jax.experimental.pallas import tpu as pltpu
from jax.sharding import PartitionSpec as P

MIB = 1024 * 1024
LANES = 128
WIDE = 256
SLOTS = 4
TOKEN = jax.ShapeDtypeStruct((8, LANES), jnp.float32)
SIZES = (32, 32, 32, 32)
FETCHES = (1, 1, 2)
RETURNS = ((0, 2), (2, 3), (3, 4))

IN_VMEM = pl.BlockSpec(memory_space=pltpu.VMEM)
IN_SMEM = pl.BlockSpec(memory_space=pltpu.SMEM)
ANYWHERE = pl.BlockSpec(memory_space=pl.ANY)


def shifted(value, axis, steps):
    count = lax.axis_size(axis)
    first, last = (max(0, -steps), min(count, count - steps))
    return lax.ppermute(value, axis, [(source, source + steps) for source in range(first, last)])


def swapped(value, axis, bit):
    count = lax.axis_size(axis)
    return lax.ppermute(value, axis, [(source, source ^ bit) for source in range(count)])


def gathered(own, axis):
    bit = lax.axis_size(axis) // 2
    pieces = {0: own}
    while bit:
        for d in list(pieces):
            pieces[d ^ bit] = swapped(pieces[d], axis, bit)
        bit //= 2
    return [pieces[d] for d in range(len(pieces))]


def in_hbm(*values):
    return [pltpu.with_memory_space_constraint(value, pltpu.HBM) for value in values]


def in_vmem(*values):
    return [pltpu.with_memory_space_constraint(value, pltpu.VMEM) for value in values]


def halves(x):
    hi = x.astype(jnp.bfloat16)
    lo = (x - hi.astype(jnp.float32)).astype(jnp.bfloat16)
    return hi, lo


def product(both, w_hi, w_lo):
    rows = both.shape[0] // 2
    wide = jnp.dot(both, w_hi, preferred_element_type=jnp.float32)
    return wide[:rows] + wide[rows:] + jnp.dot(
        both[:rows], w_lo, preferred_element_type=jnp.float32
    )


def streamed(x_hbm, buffers, sems, body):
    slots, block = buffers.shape[:2]
    steps = x_hbm.shape[0] // block

    def copy(t):
        slot = lax.rem(t, slots)
        rows = pl.ds(pl.multiple_of(t * block, block), block)
        return pltpu.make_async_copy(x_hbm.at[rows], buffers.at[slot], sems.at[slot])

    for t in range(slots - 1):
        copy(t).start()

    @pl.loop(0, steps)
    def _(t):
        @pl.when(t + slots - 1 < steps)
        def _():
            copy(t + slots - 1).start()

        copy(t).wait()
        body(t, buffers.at[lax.rem(t, slots)])


def split_core_kernel(spins, tiles, x_hbm, _, hi_ref, lo_ref, token_ref, buffers, sems):
    step = spins * tiles
    block = buffers.shape[1] // step

    def body(t, x_ref):
        rows = pl.ds(pl.multiple_of(t * block, block), block)
        for tile in range(tiles):
            for i in range(spins):
                x = x_ref[pl.ds(tile * spins + i, block, stride=step), :]
                hi, lo = halves(x)
                lanes = slice(tile * LANES, (tile + 1) * LANES)
                hi_ref[i, rows, lanes] = hi
                lo_ref[i, rows, lanes] = lo

    streamed(x_hbm, buffers, sems, body)
    token_ref[...] = jnp.zeros_like(token_ref)


def split_core(core, after):
    bond, spins, cols = core.shape
    tiles = cols // LANES
    step = spins * tiles
    block = bond // 8
    flat = core.reshape(bond, spins, tiles, LANES).transpose(0, 2, 1, 3).reshape(bond * step, LANES)
    flat = pltpu.with_memory_space_constraint(flat, pltpu.HBM)
    out = pltpu.VMEM((spins, bond, cols), jnp.bfloat16)
    return pl.pallas_call(
        functools.partial(split_core_kernel, spins, tiles),
        in_specs=[ANYWHERE, ANYWHERE],
        out_specs=[IN_VMEM] * 3,
        out_shape=[out, out, TOKEN],
        scratch_shapes=[
            pltpu.VMEM((SLOTS, block * step, LANES), jnp.float32),
            pltpu.SemaphoreType.DMA((SLOTS,)),
        ],
        compiler_params=pltpu.CompilerParams(vmem_limit_bytes=8 * MIB),
        cost_estimate=pl.CostEstimate(
            flops=4 * core.size, bytes_accessed=8 * core.size, transcendentals=0
        ),
        name="split_core",
    )(flat, after)


def split_left_kernel(spins, tiles, x_ref, _, hi_ref, lo_ref, token_ref):
    rows, wide = hi_ref.shape[1:]
    blocks = hi_ref.shape[0] // spins
    for tile in range(tiles):
        at, lane = divmod(tile * LANES, wide)
        for i in range(spins):
            x = x_ref[pl.ds(tile * spins + i, rows, stride=spins * tiles), :]
            hi, lo = halves(x)
            hi_ref[i * blocks + at, :, lane:lane + LANES] = hi
            lo_ref[i * blocks + at, :, lane:lane + LANES] = lo
    token_ref[...] = jnp.zeros_like(token_ref)


def split_left(core, after):
    bond, spins, cols = core.shape
    tiles = cols // LANES
    wide = min(WIDE, cols)
    step = spins * tiles
    block = bond // 8
    flat = core.reshape(bond, spins, tiles, LANES).transpose(0, 2, 1, 3).reshape(bond * step, LANES)
    flat = pltpu.with_memory_space_constraint(flat, pltpu.HBM)
    blocks = spins * cols // wide
    out = pltpu.HBM((blocks, bond, wide), jnp.bfloat16)
    out_spec = pl.BlockSpec((blocks, block, wide), lambda t: (0, t, 0))
    return pl.pallas_call(
        functools.partial(split_left_kernel, spins, tiles),
        grid=(bond // block,),
        in_specs=[pl.BlockSpec((block * step, LANES), lambda t: (t, 0)), ANYWHERE],
        out_specs=[out_spec, out_spec, pl.BlockSpec(TOKEN.shape, lambda t: (0, 0))],
        out_shape=[out, out, TOKEN],
        compiler_params=pltpu.CompilerParams(vmem_limit_bytes=8 * MIB),
        cost_estimate=pl.CostEstimate(
            flops=4 * core.size, bytes_accessed=8 * core.size, transcendentals=0
        ),
        name="split_left",
    )(flat, after)


def split_env_kernel(x_hbm, _, hi_ref, lo_ref, token_ref, buffers, sems):
    block = buffers.shape[1]

    def body(t, x_ref):
        rows = pl.ds(pl.multiple_of(t * block, block), block)
        hi_ref[rows, :], lo_ref[rows, :] = halves(x_ref[...])

    streamed(x_hbm, buffers, sems, body)
    token_ref[...] = jnp.zeros_like(token_ref)


def split_env(env, after):
    rows, cols = env.shape
    block = 128
    env = pltpu.with_memory_space_constraint(env, pltpu.HBM)
    out = pltpu.VMEM((rows, cols), jnp.bfloat16)
    return pl.pallas_call(
        split_env_kernel,
        in_specs=[ANYWHERE, ANYWHERE],
        out_specs=[IN_VMEM] * 3,
        out_shape=[out, out, TOKEN],
        scratch_shapes=[
            pltpu.VMEM((SLOTS, block, cols), jnp.float32),
            pltpu.SemaphoreType.DMA((SLOTS,)),
        ],
        compiler_params=pltpu.CompilerParams(vmem_limit_bytes=8 * MIB),
        cost_estimate=pl.CostEstimate(
            flops=4 * env.size, bytes_accessed=4 * env.size, transcendentals=0
        ),
        name="split_env",
    )(env, after)


def lay_out(row, pieces, both_ref):
    rows = both_ref.shape[0] // 2
    for d, x in enumerate(pieces):
        cols = x.shape[-1]
        hi, lo = halves(x.reshape(rows, cols))
        at = pl.ds(pl.multiple_of((row ^ d) * cols, cols), cols)
        both_ref[:rows, at] = hi
        both_ref[rows:, at] = lo


def cut_kernel(start, env_hbm, _, out_ref, sem):
    rows = pl.ds(start, out_ref.shape[1])
    copy = pltpu.make_async_copy(env_hbm.at[:, rows, :], out_ref, sem)
    copy.start()
    copy.wait()


def cut(env, start, size, after):
    width, _, cols = env.shape
    return pl.pallas_call(
        functools.partial(cut_kernel, start),
        in_specs=[ANYWHERE, ANYWHERE],
        out_specs=IN_VMEM,
        out_shape=pltpu.VMEM((width, size, cols), env.dtype),
        scratch_shapes=[pltpu.SemaphoreType.DMA(())],
        compiler_params=pltpu.CompilerParams(vmem_limit_bytes=4 * MIB),
        name="cut",
    )(pltpu.with_memory_space_constraint(env, pltpu.HBM), after)


def copied_kernel(x_ref, _, out_ref):
    out_ref[...] = x_ref[...]


def copied(x, after):
    return pl.pallas_call(
        copied_kernel,
        in_specs=[IN_VMEM, ANYWHERE],
        out_specs=IN_VMEM,
        out_shape=jax.ShapeDtypeStruct(x.shape, x.dtype),
        compiler_params=pltpu.CompilerParams(vmem_limit_bytes=4 * MIB),
        name="copied",
    )(x, after)


def left_kernel(count, starts, panel, row_ref, mpo_ref, _, *refs):
    pieces = refs[:count]
    hi_hbm, lo_hbm, inv_ref, out_ref, both_ref, acc_ref, hi_ref, lo_ref, sems = refs[count:]
    width, _, cols = pieces[0].shape
    spins = acc_ref.shape[0]
    wide = hi_ref.shape[2]
    copies = [
        [
            pltpu.make_async_copy(source.at[n], target.at[n % 2], sems.at[k, n % 2])
            for k, (source, target) in enumerate(((hi_hbm, hi_ref), (lo_hbm, lo_ref)))
        ]
        for n in range(hi_hbm.shape[0])
    ]
    for pair in copies[:2]:
        for copy in pair:
            copy.start()
    lay_out(
        row_ref[0],
        [ref[:, start:start + panel, :] for ref, start in zip(pieces, starts)],
        both_ref,
    )
    for n, pair in enumerate(copies):
        i, c = divmod(n * wide, cols)
        for copy in pair:
            copy.wait()
        acc_ref[i, :, c:c + wide] = product(both_ref[...], hi_ref[n % 2], lo_ref[n % 2])
        for copy in [copy for pair in copies[n + 2:n + 3] for copy in pair]:
            copy.start()
    for c in range(0, cols, wide):
        at = slice(c, c + wide)
        inv = inv_ref[:, at]
        for p in range(2):
            for y in range(width):
                total = None
                for w in range(width):
                    for i in range(spins):
                        scalar = mpo_ref[((w * width + y) * 2 + p) * 2 + i]
                        value = scalar * acc_ref[i, w * panel:(w + 1) * panel, at]
                        total = value if total is None else total + value
                out_ref[p * width + y, :, at] = total * inv


def left_block(row, mpo, after, pieces, starts, panel, core_hi, core_lo, inv):
    width, _, cols = pieces[0].shape
    blocks, bond, wide = core_hi.shape
    spins = blocks * wide // cols
    count = len(pieces)
    macs = width * panel * bond * spins * cols
    return pl.pallas_call(
        functools.partial(left_kernel, count, starts, panel),
        in_specs=[IN_SMEM] * 2
        + [ANYWHERE]
        + [IN_VMEM] * count
        + [ANYWHERE] * 2
        + [IN_VMEM],
        out_specs=IN_VMEM,
        out_shape=jax.ShapeDtypeStruct((2 * width, panel, cols), jnp.float32),
        scratch_shapes=[
            pltpu.VMEM((2 * width * panel, bond), jnp.bfloat16),
            pltpu.VMEM((spins, width * panel, cols), jnp.float32),
            pltpu.VMEM((2, bond, wide), core_hi.dtype),
            pltpu.VMEM((2, bond, wide), core_lo.dtype),
            pltpu.SemaphoreType.DMA((2, 2)),
        ],
        compiler_params=pltpu.CompilerParams(vmem_limit_bytes=8 * MIB),
        cost_estimate=pl.CostEstimate(
            flops=8 * macs, bytes_accessed=0, transcendentals=0
        ),
        name="left_block",
    )(row, mpo, after, *pieces, *in_hbm(core_hi, core_lo), inv)


def right_kernel(count, row_ref, mpo_ref, _, *refs):
    pieces = refs[:count]
    core_hi, core_lo, env_hi, env_lo, send_ref, keep_ref = refs[count:count + 6]
    both_ref, first_ref, mixed_ref = refs[count + 6:]
    row = row_ref[0]
    blocks, panel, cols = pieces[0].shape
    width = blocks // 2
    spins = core_hi.shape[0]
    wide = min(WIDE, cols)
    lay_out(row, [ref[...] for ref in pieces], both_ref)
    for c in range(0, cols, wide):
        at = slice(c, c + wide)
        for j in range(spins):
            first_ref[j, :, at] = product(both_ref[...], core_hi[j, :, at], core_lo[j, :, at])
    for c in range(0, cols, wide):
        at = slice(c, c + wide)
        for p in range(2):
            for q in range(2):
                to = (p * 2 + q) * panel
                for z in range(width):
                    total = None
                    for y in range(width):
                        for j in range(spins):
                            scalar = mpo_ref[((y * width + z) * 2 + q) * 2 + j]
                            start = (p * width + y) * panel
                            value = scalar * first_ref[j, start:start + panel, at]
                            total = value if total is None else total + value
                    hi, lo = halves(total)
                    lanes = slice(z * cols + c, z * cols + c + wide)
                    mixed_ref[to:to + panel, lanes] = hi
                    mixed_ref[4 * panel + to:5 * panel + to, lanes] = lo
    for d in [*range(1, count, 2), *range(0, count, 2)]:
        out_ref = send_ref if d % 2 else keep_ref
        out_cols = out_ref.shape[2]
        wide = min(WIDE, out_cols)
        for c in range(0, out_cols, wide):
            at = pl.ds(pl.multiple_of((row ^ d) * out_cols + c, wide), wide)
            out_ref[d // 2, :, c:c + wide] = product(
                mixed_ref[...], env_hi[:, at], env_lo[:, at]
            )


def right_block(row, mpo, after, pieces, core_hi, core_lo, env_hi, env_lo):
    blocks, panel, cols = pieces[0].shape
    spins, bond, _ = core_hi.shape
    inner, outer = env_hi.shape
    count = len(pieces)
    out = jax.ShapeDtypeStruct((count // 2, 4 * panel, outer // count), jnp.float32)
    macs = blocks * panel * bond * spins * cols + 4 * panel * inner * outer
    return pl.pallas_call(
        functools.partial(right_kernel, count),
        in_specs=[IN_SMEM] * 2 + [ANYWHERE] + [IN_VMEM] * (count + 4),
        out_specs=[IN_VMEM, IN_VMEM],
        out_shape=[out, out],
        scratch_shapes=[
            pltpu.VMEM((2 * blocks * panel, bond), jnp.bfloat16),
            pltpu.VMEM((spins, blocks * panel, cols), jnp.float32),
            pltpu.VMEM((8 * panel, inner), jnp.bfloat16),
        ],
        compiler_params=pltpu.CompilerParams(vmem_limit_bytes=14 * MIB),
        cost_estimate=pl.CostEstimate(
            flops=8 * macs, bytes_accessed=0, transcendentals=0
        ),
        name="right_block",
    )(row, mpo, after, *pieces, *in_vmem(core_hi, core_lo, env_hi, env_lo))


def per_device(left_env, left_core, inv_sing, mpo_pair, right_core, right_env):
    count = lax.axis_size("row")
    row = lax.axis_index("row").astype(jnp.int32).reshape(1)
    env = left_env[0].transpose(1, 0, 2)
    mpo_left = mpo_pair[0, 0].reshape(-1)
    mpo_right = shifted(mpo_pair[0, 1].reshape(-1), "seg", 1)
    inner = right_env.shape[1] * right_env.shape[2]

    *core_a, first = split_left(left_core[0], mpo_right)
    fetched = []
    begin = 0
    after = row
    for number in FETCHES:
        sizes = SIZES[len(fetched):len(fetched) + number]
        own = cut(env, begin, sum(sizes), after)
        bit = count // 2
        pieces = {0: own}
        while bit:
            for d in list(pieces):
                value = pieces[d]
                if d and not fetched:
                    value = copied(value, first)
                pieces[d ^ bit] = swapped(value, "row", bit)
            bit //= 2
        pieces = [pieces[d] for d in range(count)]
        after = pieces[count // 2]
        start = 0
        for size in sizes:
            fetched.append((pieces, start, size))
            start += size
        begin += start

    sent = []
    after = first
    for k, (pieces, start, size) in enumerate(fetched):
        if k == 2:
            *core_b, after = split_core(right_core[0], after)
        after = left_block(
            row, mpo_left, after, pieces, [start] * count, size, *core_a, inv_sing
        )
        sent.append(shifted(after, "seg", 1))

    flat = right_env[0].reshape(inner, right_env.shape[3])
    *env_b, after = split_env(flat, after)
    totals = []
    for scaled in sent:
        pieces = gathered(scaled, "row")
        send, keep = right_block(row, mpo_right, after, pieces, *core_b, *env_b)
        after = send
        came = swapped(send, "row", 1)
        sums = [keep[m] + came[m] for m in range(count // 2)]
        bit = 2
        while len(sums) > 1:
            came = [swapped(value, "row", bit) for value in sums[1::2]]
            sums = [one + two for one, two in zip(sums[0::2], came)]
            bit *= 2
        totals.append(sums[0])

    outs = []
    for first, last in RETURNS:
        back = shifted(jnp.stack(totals[first:last]), "seg", -1)
        for size, rows in zip(SIZES[first:last], back):
            outs.append(rows.reshape(2, 2, size, rows.shape[1]).transpose(2, 0, 1, 3))
    return jnp.concatenate(outs, 0)[None]


def solution(mesh):
    return jax.shard_map(
        per_device,
        mesh=mesh,
        in_specs=(
            P("seg", None, None, "row"),
            P("seg", None, None, "row"),
            P("seg", "row"),
            P("seg", None, None, None, None, None),
            P("seg", None, None, "row"),
            P("seg", None, "row", None),
        ),
        out_specs=P("seg", None, None, None, "row"),
        check_vma=False,
    )
```

```python
import jax
import jax.numpy as jnp
from jax import lax
from jax.experimental import pallas as pl
from jax.experimental.pallas import tpu as pltpu
from jax.sharding import PartitionSpec as P

MIB = 1024 * 1024
LANES = 128
WIDE = 256
SLOTS = 4
TOKEN = jax.ShapeDtypeStruct((8, LANES), jnp.float32)
COST = 2 * 10**9
SIZES = (32, 32, 32, 32)
FETCHES = (1, 1, 2)

def shifted(value, axis, steps):
    count = lax.axis_size(axis)
    first, last = (max(0, -steps), min(count, count - steps))
    return lax.ppermute(value, axis, [(source, source + steps) for source in range(first, last)])


def swapped(value, axis, bit):
    count = lax.axis_size(axis)
    return lax.ppermute(value, axis, [(source, source ^ bit) for source in range(count)])


def in_vmem(value):
    return pltpu.with_memory_space_constraint(value, pltpu.VMEM)


def in_hbm(value):
    return pltpu.with_memory_space_constraint(value, pltpu.HBM)


VMEM, SMEM, ANY = (
    pl.BlockSpec(memory_space=space) for space in (pltpu.VMEM, pltpu.SMEM, pl.ANY)
)


def run(name, vmem, after, *parts):
    inputs = [pair for part in parts for pair in part[1]]
    waits = len(after)
    outs = [shape for part in parts for shape in part[2]]
    groups = {id(part[3]): part[3] for part in parts}
    places = dict(zip(groups, [sum(map(len, list(groups.values())[:n])) for n in range(len(groups))]))
    scratch = [shape for group in groups.values() for shape in group]

    def kernel(*refs):
        refs = list(refs)
        ins, refs = refs[:len(inputs)], refs[len(inputs) + waits:]
        results, own = refs[:len(outs)], refs[len(outs):]
        for part in parts:
            taken = []
            for group, number in ((ins, len(part[1])), (results, len(part[2]))):
                taken += group[:number]
                del group[:number]
            place = places[id(part[3])]
            part[0](*taken, *own[place:place + len(part[3])])

    values = pl.pallas_call(
        kernel,
        in_specs=[spec for spec, _ in inputs] + [ANY] * waits,
        out_specs=[VMEM] * len(outs),
        out_shape=outs,
        scratch_shapes=scratch,
        compiler_params=pltpu.CompilerParams(vmem_limit_bytes=vmem * MIB),
        cost_estimate=pl.CostEstimate(flops=COST, bytes_accessed=0, transcendentals=0),
        name=name,
    )(*[value for _, value in inputs], *after)
    values = list(values)
    result = []
    for part in parts:
        result.append(values[:len(part[2])])
        del values[:len(part[2])]
    return result

def halves(x):
    hi = x.astype(jnp.bfloat16)
    lo = (x - hi.astype(jnp.float32)).astype(jnp.bfloat16)
    return hi, lo


def product(both, w_hi, w_lo):
    rows = both.shape[0] // 2
    wide = jnp.dot(both, w_hi, preferred_element_type=jnp.float32)
    return wide[:rows] + wide[rows:] + jnp.dot(
        both[:rows], w_lo, preferred_element_type=jnp.float32
    )


def streamed(x_hbm, buffers, sems, body):
    slots, block = buffers.shape[:2]
    steps = x_hbm.shape[0] // block

    def copy(t):
        slot = lax.rem(t, slots)
        rows = pl.ds(pl.multiple_of(t * block, block), block)
        return pltpu.make_async_copy(x_hbm.at[rows], buffers.at[slot], sems.at[slot])

    for t in range(slots - 1):
        copy(t).start()

    @pl.loop(0, steps)
    def _(t):
        @pl.when(t + slots - 1 < steps)
        def _():
            copy(t + slots - 1).start()

        copy(t).wait()
        body(t, buffers.at[lax.rem(t, slots)])


def split_core(core):
    bond, spins, cols = core.shape
    tiles = cols // LANES
    step = spins * tiles
    block = bond // 8
    flat = core.reshape(bond, spins, tiles, LANES).transpose(0, 2, 1, 3).reshape(bond * step, LANES)

    def body(x_hbm, hi_ref, lo_ref, token_ref, buffers, sems):
        def split(t, x_ref):
            rows = pl.ds(pl.multiple_of(t * block, block), block)
            for tile in range(tiles):
                lanes = slice(tile * LANES, (tile + 1) * LANES)
                for i in range(spins):
                    x = x_ref[pl.ds(tile * spins + i, block, stride=step), :]
                    hi_ref[i, rows, lanes], lo_ref[i, rows, lanes] = halves(x)

        streamed(x_hbm, buffers, sems, split)
        token_ref[...] = jnp.zeros_like(token_ref)

    out = pltpu.VMEM((spins, bond, cols), jnp.bfloat16)
    scratch = [
        pltpu.VMEM((SLOTS, block * step, LANES), jnp.float32),
        pltpu.SemaphoreType.DMA((SLOTS,)),
    ]
    return body, [(ANY, in_hbm(flat))], [out, out, TOKEN], scratch


def split_env(env):
    rows, cols = env.shape
    block = LANES

    def body(x_hbm, hi_ref, lo_ref, token_ref, buffers, sems):
        def split(t, x_ref):
            at = pl.ds(pl.multiple_of(t * block, block), block)
            hi_ref[at, :], lo_ref[at, :] = halves(x_ref[...])

        streamed(x_hbm, buffers, sems, split)
        token_ref[...] = jnp.zeros_like(token_ref)

    out = pltpu.VMEM((rows, cols), jnp.bfloat16)
    scratch = [
        pltpu.VMEM((SLOTS, block, cols), jnp.float32),
        pltpu.SemaphoreType.DMA((SLOTS,)),
    ]
    return body, [(ANY, in_hbm(env))], [out, out, TOKEN], scratch


def cut(env, start, size):
    width, _, cols = env.shape

    def body(env_hbm, out_ref, sem):
        copy = pltpu.make_async_copy(env_hbm.at[:, pl.ds(start, size), :], out_ref, sem)
        copy.start()
        copy.wait()

    out = pltpu.VMEM((width, size, cols), env.dtype)
    return body, [(ANY, in_hbm(env))], [out], [pltpu.SemaphoreType.DMA(())]


def copied(x):
    def body(x_ref, out_ref):
        out_ref[...] = x_ref[...]

    return body, [(VMEM, x)], [jax.ShapeDtypeStruct(x.shape, x.dtype)], []


def added(x, y):
    def body(x_ref, y_ref, out_ref):
        out_ref[...] = x_ref[...] + y_ref[...]

    return body, [(VMEM, x), (VMEM, y)], [jax.ShapeDtypeStruct(x.shape, x.dtype)], []


def lay_out(row, pieces, both_ref):
    rows = both_ref.shape[0] // 2
    for d, x in enumerate(pieces):
        cols = x.shape[-1]
        hi, lo = halves(x.reshape(rows, cols))
        at = pl.ds(pl.multiple_of((row ^ d) * cols, cols), cols)
        both_ref[:rows, at] = hi
        both_ref[rows:, at] = lo


def left(row, mpo, pieces, start, panel, core_hi, core_lo, inv):
    width, _, cols = pieces[0].shape
    spins, bond, _ = core_hi.shape
    count = len(pieces)
    wide = min(WIDE, cols)

    def body(row_ref, mpo_ref, *refs):
        pieces = refs[:count]
        hi_ref, lo_ref, inv_ref, out_ref, both_ref, acc_ref = refs[count:]
        lay_out(row_ref[0], [ref[:, start:start + panel, :] for ref in pieces], both_ref)

        @pl.loop(0, spins * (cols // wide))
        def _(n):
            i, at = n % spins, pl.ds(pl.multiple_of(n // spins * wide, wide), wide)
            acc_ref[i, :, at] = product(both_ref[...], hi_ref[i, :, at], lo_ref[i, :, at])

        for c in range(0, cols, wide):
            at = slice(c, c + wide)
            inv = inv_ref[:, at]
            for p in range(2):
                for y in range(width):
                    total = None
                    for w in range(width):
                        for i in range(spins):
                            scalar = mpo_ref[((w * width + y) * 2 + p) * 2 + i]
                            value = scalar * acc_ref[i, w * panel:(w + 1) * panel, at]
                            total = value if total is None else total + value
                    out_ref[p * width + y, :, at] = total * inv

    inputs = [(SMEM, row), (SMEM, mpo)] + [(VMEM, piece) for piece in pieces]
    inputs += [(VMEM, in_vmem(core_hi)), (VMEM, in_vmem(core_lo)), (VMEM, inv)]
    out = jax.ShapeDtypeStruct((2 * width, panel, cols), jnp.float32)
    scratch = [
        pltpu.VMEM((2 * width * panel, bond), jnp.bfloat16),
        pltpu.VMEM((spins, width * panel, cols), jnp.float32),
    ]
    return body, inputs, [out], scratch


def right(row, mpo, pieces, core_hi, core_lo, env_hi, env_lo):
    blocks, panel, cols = pieces[0].shape
    width = blocks // 2
    spins, bond, _ = core_hi.shape
    inner, outer = env_hi.shape
    count = len(pieces)
    half = count // 2
    out_cols = outer // count

    def body(row_ref, mpo_ref, *refs):
        pieces = refs[:count]
        core_hi, core_lo, env_hi, env_lo, send_ref, keep_ref = refs[count:count + 6]
        both_ref, first_ref, mixed_ref = refs[count + 6:]
        row = row_ref[0]
        lay_out(row, [ref[...] for ref in pieces], both_ref)
        wide = min(WIDE, cols)

        @pl.loop(0, spins * (cols // wide))
        def _(n):
            j, at = n % spins, pl.ds(pl.multiple_of(n // spins * wide, wide), wide)
            first_ref[j, :, at] = product(both_ref[...], core_hi[j, :, at], core_lo[j, :, at])

        for c in range(0, cols, wide):
            at = slice(c, c + wide)
            for p in range(2):
                for q in range(2):
                    to = (p * 2 + q) * panel
                    for z in range(width):
                        total = None
                        for y in range(width):
                            for j in range(spins):
                                scalar = mpo_ref[((y * width + z) * 2 + q) * 2 + j]
                                start = (p * width + y) * panel
                                value = scalar * first_ref[j, start:start + panel, at]
                                total = value if total is None else total + value
                        hi, lo = halves(total)
                        lanes = slice(z * cols + c, z * cols + c + wide)
                        mixed_ref[to:to + panel, lanes] = hi
                        mixed_ref[4 * panel + to:5 * panel + to, lanes] = lo
        narrow = min(WIDE, out_cols)
        for parity, out_ref in ((1, send_ref), (0, keep_ref)):

            @pl.loop(0, half * (out_cols // narrow))
            def _(n):
                m, c = n % half, pl.multiple_of(n // half * narrow, narrow)
                source = pl.multiple_of((row ^ (2 * m + parity)) * out_cols + c, narrow)
                at = pl.ds(source, narrow)
                out_ref[m, :, pl.ds(c, narrow)] = product(
                    mixed_ref[...], env_hi[:, at], env_lo[:, at]
                )

    inputs = [(SMEM, row), (SMEM, mpo)] + [(VMEM, piece) for piece in pieces]
    inputs += [(VMEM, in_vmem(value)) for value in (core_hi, core_lo, env_hi, env_lo)]
    out = jax.ShapeDtypeStruct((half, 4 * panel, out_cols), jnp.float32)
    scratch = [
        pltpu.VMEM((2 * blocks * panel, bond), jnp.bfloat16),
        pltpu.VMEM((spins, blocks * panel, cols), jnp.float32),
        pltpu.VMEM((8 * panel, inner), jnp.bfloat16),
    ]
    return body, inputs, [out, out], scratch


def reduced(send, keep, axis):
    came = swapped(send, axis, 1)
    sums = [(keep[m], came[m]) for m in range(keep.shape[0])]
    bit = 2
    while len(sums) > 1:
        came = [swapped(one + two, axis, bit) for one, two in sums[1::2]]
        sums = [(one + two, three) for (one, two), three in zip(sums[0::2], came)]
        bit *= 2
    return sums[0]


def per_device(left_env, left_core, inv_sing, mpo_pair, right_core, right_env):
    count = lax.axis_size("row")
    row = lax.axis_index("row").astype(jnp.int32).reshape(1)
    env = left_env[0].transpose(1, 0, 2)
    mpo_left = mpo_pair[0, 0].reshape(-1)
    mpo_right = shifted(mpo_pair[0, 1].reshape(-1), "seg", 1)
    flat_env = right_env[0].reshape(-1, right_env.shape[3])
    chunks = len(SIZES)

    begins = [sum(SIZES[:k]) for k in range(chunks)]
    firsts = [sum(FETCHES[:f]) for f in range(len(FETCHES))]
    fetched, spread = {}, {}

    def gathered(own, other, *after):
        if after:
            ((other,),) = run("copied", 4, after, copied(other))
        pieces = {0: own, count // 2: other}
        bit = count // 4
        while bit:
            for d in list(pieces):
                pieces[d ^ bit] = swapped(pieces[d], "row", bit)
            bit //= 2
        return [pieces[d] for d in range(count)]

    def fetch(f, *after):
        k, number = firsts[f], FETCHES[f]
        ((own,),) = run("cut", 2, after, cut(env, begins[k], sum(SIZES[k:k + number])))
        fetched[f] = own, swapped(own, "row", count // 2)

    def left_part(k, *after):
        f = max(f for f in range(len(FETCHES)) if firsts[f] <= k)
        if f not in spread:
            spread[f] = gathered(*fetched[f], *after)
        return left(
            row, mpo_left, spread[f], begins[k] - begins[firsts[f]], SIZES[k], *core_a, inv_sing
        )

    fetch(0)
    (((*core_a, token)),) = run("split_a", 10, [], split_core(left_core[0]))
    fetch(1, fetched[0][1], token)
    ((scaled,),) = run("left_0", 10, [mpo_right], left_part(0))
    sent, crossed, sums = {}, {}, {}

    def send_on(k, value):
        sent[k] = shifted(value, "seg", 1)

    def cross(k, *after):
        if after:
            ((sent[k],),) = run("copied", 4, after, copied(sent[k]))
        crossed[k] = swapped(sent[k], "row", count // 2)

    def right_part(k, *after):
        return right(row, mpo_right, gathered(sent[k], crossed[k], *after), *core_b, *env_b)

    send_on(0, scaled)
    fetch(2, fetched[1][1], scaled)
    part = left_part(1)
    (scaled,), (*core_b, token) = run("left_1", 14, [scaled], part, split_core(right_core[0]))
    send_on(1, scaled)
    cross(0)
    after = [scaled, token, sent[0], fetched[2][1]]
    parts = [left_part(k, scaled) for k in range(2, chunks)]
    largest = max(parts, key=lambda part: part[3][0].shape)[3]
    parts = [part[:3] + (largest,) if part[3][0].shape == largest[0].shape else part for part in parts]
    (*env_b, token), *rest = run("left_2", 13, after, split_env(flat_env), *parts)
    for k, (scaled,) in enumerate(rest, 2):
        send_on(k, scaled)
    cross(1, token)
    outs = []

    def give_back(first, last, *after):
        results = run("added", 4, after, *[added(*reduced(*sums[k], "row")) for k in range(first, last)])
        rows = jnp.concatenate([value for (value,) in results])
        rows = shifted(rows, "seg", -1)
        begin = 0
        for size in SIZES[first:last]:
            own = rows[begin:begin + 4 * size]
            begin += 4 * size
            outs.append(own.reshape(2, 2, size, own.shape[1]).transpose(2, 0, 1, 3))
        return rows

    for k in range(chunks):
        if k == chunks - 1:
            early = give_back(0, chunks - 3)
        after = [token if k == 0 else send]
        part = right_part(k, *after)
        ((send, keep),) = run(f"right_{k}", 15, after, part)
        sums[k] = send, keep
        if k + 2 < chunks:
            cross(k + 2, send)
    give_back(chunks - 3, chunks - 1, early, send)
    give_back(chunks - 1, chunks)
    return jnp.concatenate(outs, 0)[None]


def solution(mesh):
    return jax.shard_map(
        per_device,
        mesh=mesh,
        in_specs=(
            P("seg", None, None, "row"),
            P("seg", None, None, "row"),
            P("seg", "row"),
            P("seg", None, None, None, None, None),
            P("seg", None, None, "row"),
            P("seg", None, "row", None),
        ),
        out_specs=P("seg", None, None, None, "row"),
        check_vma=False,
    )
```

```python
import jax
import jax.numpy as jnp
from jax import lax
from jax.experimental import pallas as pl
from jax.experimental.pallas import tpu as pltpu
from jax.sharding import PartitionSpec as P

MIB = 1024 * 1024
LANES = 128
WIDE = 256
SLOTS = 4
TOKEN = jax.ShapeDtypeStruct((8, LANES), jnp.float32)
COST = 2 * 10**9
SIZES = (32, 32, 32, 16, 16)
FETCHES = (1, 1, 3)

def shifted(value, axis, steps):
    count = lax.axis_size(axis)
    first, last = (max(0, -steps), min(count, count - steps))
    return lax.ppermute(value, axis, [(source, source + steps) for source in range(first, last)])


def swapped(value, axis, bit):
    count = lax.axis_size(axis)
    return lax.ppermute(value, axis, [(source, source ^ bit) for source in range(count)])


def in_vmem(value):
    return pltpu.with_memory_space_constraint(value, pltpu.VMEM)


def in_hbm(value):
    return pltpu.with_memory_space_constraint(value, pltpu.HBM)


VMEM, SMEM, ANY = (
    pl.BlockSpec(memory_space=space) for space in (pltpu.VMEM, pltpu.SMEM, pl.ANY)
)


def run(name, vmem, after, *parts):
    inputs = [pair for part in parts for pair in part[1]]
    waits = len(after)
    outs = [shape for part in parts for shape in part[2]]
    groups = {id(part[3]): part[3] for part in parts}
    places = dict(zip(groups, [sum(map(len, list(groups.values())[:n])) for n in range(len(groups))]))
    scratch = [shape for group in groups.values() for shape in group]

    def kernel(*refs):
        refs = list(refs)
        ins, refs = refs[:len(inputs)], refs[len(inputs) + waits:]
        results, own = refs[:len(outs)], refs[len(outs):]
        for part in parts:
            taken = []
            for group, number in ((ins, len(part[1])), (results, len(part[2]))):
                taken += group[:number]
                del group[:number]
            place = places[id(part[3])]
            part[0](*taken, *own[place:place + len(part[3])])

    values = pl.pallas_call(
        kernel,
        in_specs=[spec for spec, _ in inputs] + [ANY] * waits,
        out_specs=[VMEM] * len(outs),
        out_shape=outs,
        scratch_shapes=scratch,
        compiler_params=pltpu.CompilerParams(vmem_limit_bytes=vmem * MIB),
        cost_estimate=pl.CostEstimate(flops=COST, bytes_accessed=0, transcendentals=0),
        name=name,
    )(*[value for _, value in inputs], *after)
    values = list(values)
    result = []
    for part in parts:
        result.append(values[:len(part[2])])
        del values[:len(part[2])]
    return result

def halves(x):
    hi = x.astype(jnp.bfloat16)
    lo = (x - hi.astype(jnp.float32)).astype(jnp.bfloat16)
    return hi, lo


def product(both, w_hi, w_lo):
    rows = both.shape[0] // 2
    wide = jnp.dot(both, w_hi, preferred_element_type=jnp.float32)
    return wide[:rows] + wide[rows:] + jnp.dot(
        both[:rows], w_lo, preferred_element_type=jnp.float32
    )


def streamed(x_hbm, buffers, sems, body):
    slots, block = buffers.shape[:2]
    steps = x_hbm.shape[0] // block

    def copy(t):
        slot = lax.rem(t, slots)
        rows = pl.ds(pl.multiple_of(t * block, block), block)
        return pltpu.make_async_copy(x_hbm.at[rows], buffers.at[slot], sems.at[slot])

    for t in range(slots - 1):
        copy(t).start()

    @pl.loop(0, steps)
    def _(t):
        @pl.when(t + slots - 1 < steps)
        def _():
            copy(t + slots - 1).start()

        copy(t).wait()
        body(t, buffers.at[lax.rem(t, slots)])


def split_core(core):
    bond, spins, cols = core.shape
    tiles = cols // LANES
    step = spins * tiles
    block = bond // 8
    flat = core.reshape(bond, spins, tiles, LANES).transpose(0, 2, 1, 3).reshape(bond * step, LANES)

    def body(x_hbm, hi_ref, lo_ref, token_ref, buffers, sems):
        def split(t, x_ref):
            rows = pl.ds(pl.multiple_of(t * block, block), block)
            for tile in range(tiles):
                lanes = slice(tile * LANES, (tile + 1) * LANES)
                for i in range(spins):
                    x = x_ref[pl.ds(tile * spins + i, block, stride=step), :]
                    hi_ref[i, rows, lanes], lo_ref[i, rows, lanes] = halves(x)

        streamed(x_hbm, buffers, sems, split)
        token_ref[...] = jnp.zeros_like(token_ref)

    out = pltpu.VMEM((spins, bond, cols), jnp.bfloat16)
    scratch = [
        pltpu.VMEM((SLOTS, block * step, LANES), jnp.float32),
        pltpu.SemaphoreType.DMA((SLOTS,)),
    ]
    return body, [(ANY, in_hbm(flat))], [out, out, TOKEN], scratch


def split_env(env):
    rows, cols = env.shape
    block = LANES

    def body(x_hbm, hi_ref, lo_ref, token_ref, buffers, sems):
        def split(t, x_ref):
            at = pl.ds(pl.multiple_of(t * block, block), block)
            hi_ref[at, :], lo_ref[at, :] = halves(x_ref[...])

        streamed(x_hbm, buffers, sems, split)
        token_ref[...] = jnp.zeros_like(token_ref)

    out = pltpu.VMEM((rows, cols), jnp.bfloat16)
    scratch = [
        pltpu.VMEM((SLOTS, block, cols), jnp.float32),
        pltpu.SemaphoreType.DMA((SLOTS,)),
    ]
    return body, [(ANY, in_hbm(env))], [out, out, TOKEN], scratch


def cut(env, start, size):
    width, _, cols = env.shape

    def body(env_hbm, out_ref, sem):
        copy = pltpu.make_async_copy(env_hbm.at[:, pl.ds(start, size), :], out_ref, sem)
        copy.start()
        copy.wait()

    out = pltpu.VMEM((width, size, cols), env.dtype)
    return body, [(ANY, in_hbm(env))], [out], [pltpu.SemaphoreType.DMA(())]


def copied(x):
    def body(x_ref, out_ref):
        out_ref[...] = x_ref[...]

    return body, [(VMEM, x)], [jax.ShapeDtypeStruct(x.shape, x.dtype)], []


def added(*pairs):
    rows = [x.shape[0] for x, _ in pairs]

    def body(*refs):
        for n in range(len(pairs)):
            at = slice(sum(rows[:n]), sum(rows[:n + 1]))
            refs[-1][at, :] = refs[2 * n][...] + refs[2 * n + 1][...]

    x = pairs[0][0]
    out = jax.ShapeDtypeStruct((sum(rows), x.shape[1]), x.dtype)
    return body, [(VMEM, value) for pair in pairs for value in pair], [out], []


def lay_out(row, pieces, both_ref):
    rows = both_ref.shape[0] // 2
    for d, x in enumerate(pieces):
        cols = x.shape[-1]
        hi, lo = halves(x.reshape(rows, cols))
        at = pl.ds(pl.multiple_of((row ^ d) * cols, cols), cols)
        both_ref[:rows, at] = hi
        both_ref[rows:, at] = lo


def left(row, mpo, pieces, start, panel, core_hi, core_lo, inv):
    width, _, cols = pieces[0].shape
    spins, bond, _ = core_hi.shape
    count = len(pieces)
    wide = min(WIDE, cols)

    def body(row_ref, mpo_ref, *refs):
        pieces = refs[:count]
        hi_ref, lo_ref, inv_ref, out_ref, both_ref, acc_ref = refs[count:]
        lay_out(row_ref[0], [ref[:, start:start + panel, :] for ref in pieces], both_ref)

        @pl.loop(0, spins * (cols // wide))
        def _(n):
            i, at = n % spins, pl.ds(pl.multiple_of(n // spins * wide, wide), wide)
            acc_ref[i, :, at] = product(both_ref[...], hi_ref[i, :, at], lo_ref[i, :, at])

        for c in range(0, cols, wide):
            at = slice(c, c + wide)
            inv = inv_ref[:, at]
            for p in range(2):
                for y in range(width):
                    total = None
                    for w in range(width):
                        for i in range(spins):
                            scalar = mpo_ref[((w * width + y) * 2 + p) * 2 + i]
                            value = scalar * acc_ref[i, w * panel:(w + 1) * panel, at]
                            total = value if total is None else total + value
                    out_ref[p * width + y, :, at] = total * inv

    inputs = [(SMEM, row), (SMEM, mpo)] + [(VMEM, piece) for piece in pieces]
    inputs += [(VMEM, in_vmem(core_hi)), (VMEM, in_vmem(core_lo)), (VMEM, inv)]
    out = jax.ShapeDtypeStruct((2 * width, panel, cols), jnp.float32)
    scratch = [
        pltpu.VMEM((2 * width * panel, bond), jnp.bfloat16),
        pltpu.VMEM((spins, width * panel, cols), jnp.float32),
    ]
    return body, inputs, [out], scratch


def right(row, mpo, pieces, core_hi, core_lo, env_hi, env_lo):
    blocks, panel, cols = pieces[0].shape
    width = blocks // 2
    spins, bond, _ = core_hi.shape
    inner, outer = env_hi.shape
    count = len(pieces)
    half = count // 2
    out_cols = outer // count

    def body(row_ref, mpo_ref, *refs):
        pieces = refs[:count]
        core_hi, core_lo, env_hi, env_lo, send_ref, keep_ref = refs[count:count + 6]
        both_ref, first_ref, mixed_ref = refs[count + 6:]
        row = row_ref[0]
        lay_out(row, [ref[...] for ref in pieces], both_ref)
        wide = min(WIDE, cols)

        for c in range(0, cols, wide):
            at = slice(c, c + wide)
            for j in range(spins):
                first_ref[j, :, at] = product(
                    both_ref[...], core_hi[j, :, at], core_lo[j, :, at]
                )
        for c in range(0, cols, wide):
            at = slice(c, c + wide)
            for p in range(2):
                for q in range(2):
                    to = (p * 2 + q) * panel
                    for z in range(width):
                        total = None
                        for y in range(width):
                            for j in range(spins):
                                scalar = mpo_ref[((y * width + z) * 2 + q) * 2 + j]
                                start = (p * width + y) * panel
                                value = scalar * first_ref[j, start:start + panel, at]
                                total = value if total is None else total + value
                        hi, lo = halves(total)
                        lanes = slice(z * cols + c, z * cols + c + wide)
                        mixed_ref[to:to + panel, lanes] = hi
                        mixed_ref[4 * panel + to:5 * panel + to, lanes] = lo
        narrow = min(WIDE, out_cols)
        for d in [*range(1, count, 2), *range(0, count, 2)]:
            out_ref = send_ref if d % 2 else keep_ref
            for c in range(0, out_cols, narrow):
                at = pl.ds(pl.multiple_of((row ^ d) * out_cols + c, narrow), narrow)
                out_ref[d // 2, :, c:c + narrow] = product(
                    mixed_ref[...], env_hi[:, at], env_lo[:, at]
                )

    inputs = [(SMEM, row), (SMEM, mpo)] + [(VMEM, piece) for piece in pieces]
    inputs += [(VMEM, in_vmem(value)) for value in (core_hi, core_lo, env_hi, env_lo)]
    out = jax.ShapeDtypeStruct((half, 4 * panel, out_cols), jnp.float32)
    scratch = [
        pltpu.VMEM((2 * blocks * panel, bond), jnp.bfloat16),
        pltpu.VMEM((spins, blocks * panel, cols), jnp.float32),
        pltpu.VMEM((8 * panel, inner), jnp.bfloat16),
    ]
    return body, inputs, [out, out], scratch


def reduced(send, keep, axis):
    came = swapped(send, axis, 1)
    sums = [(keep[m], came[m]) for m in range(keep.shape[0])]
    bit = 2
    while len(sums) > 1:
        values = [value for (value,) in run("added", 4, [], *[added(pair) for pair in sums])]
        came = [swapped(value, axis, bit) for value in values[1::2]]
        sums = list(zip(values[0::2], came))
        bit *= 2
    return sums[0]


def per_device(left_env, left_core, inv_sing, mpo_pair, right_core, right_env):
    count = lax.axis_size("row")
    row = lax.axis_index("row").astype(jnp.int32).reshape(1)
    env = left_env[0].transpose(1, 0, 2)
    mpo_left = mpo_pair[0, 0].reshape(-1)
    mpo_sent = mpo_pair[0, 1].reshape(-1)
    mpo_right = shifted(mpo_sent, "seg", 1)
    flat_env = right_env[0].reshape(-1, right_env.shape[3])
    chunks = len(SIZES)

    begins = [sum(SIZES[:k]) for k in range(chunks)]
    firsts = [sum(FETCHES[:f]) for f in range(len(FETCHES))]
    fetched, spread = {}, {}

    def gathered(own, other, *after):
        if after:
            ((other,),) = run("copied", 4, after, copied(other))
        pieces = {0: own, count // 2: other}
        bit = count // 4
        while bit:
            for d in list(pieces):
                pieces[d ^ bit] = swapped(pieces[d], "row", bit)
            bit //= 2
        return [pieces[d] for d in range(count)]

    def fetch(f, *after):
        k, number = firsts[f], FETCHES[f]
        ((own,),) = run("cut", 2, after, cut(env, begins[k], sum(SIZES[k:k + number])))
        fetched[f] = own, swapped(own, "row", count // 2)

    def left_part(k, *after):
        f = max(f for f in range(len(FETCHES)) if firsts[f] <= k)
        if f not in spread:
            spread[f] = gathered(*fetched[f], *after)
        return left(
            row, mpo_left, spread[f], begins[k] - begins[firsts[f]], SIZES[k], *core_a, inv_sing
        )

    fetch(0)
    (((*core_a, token)),) = run("split_a", 10, [mpo_left, mpo_sent], split_core(left_core[0]))
    fetch(1, fetched[0][1], token)
    ((scaled,),) = run("left_0", 10, [], left_part(0))
    sent, crossed, sums = {}, {}, {}

    def send_on(k, value):
        sent[k] = shifted(value, "seg", 1)

    def cross(k, *after):
        if after:
            ((sent[k],),) = run("copied", 4, after, copied(sent[k]))
        crossed[k] = swapped(sent[k], "row", count // 2)

    def right_part(k, *after):
        return right(row, mpo_right, gathered(sent[k], crossed[k], *after), *core_b, *env_b)

    send_on(0, scaled)
    fetch(2, fetched[1][1], scaled)
    part = left_part(1)
    (scaled,), (*core_b, token) = run("left_1", 14, [scaled], part, split_core(right_core[0]))
    send_on(1, scaled)
    cross(0)
    after = [scaled, token, sent[0], fetched[2][1]]
    parts = [left_part(k, scaled, mpo_right) for k in range(2, chunks)]
    scratches = {part[3][0].shape: part[3] for part in parts}
    parts = [part[:3] + (scratches[part[3][0].shape],) for part in parts]
    (*env_b, token), *rest = run("left_2", 14, after, split_env(flat_env), *parts)
    for k, (scaled,) in enumerate(rest, 2):
        send_on(k, scaled)
    cross(1, token)
    outs = []

    def give_back(first, last, *after):
        pairs = [reduced(*sums[k], "row") for k in range(first, last)]
        ((rows,),) = run("added", 4, after, added(*pairs))
        rows = shifted(rows, "seg", -1)
        begin = 0
        for size in SIZES[first:last]:
            own = rows[begin:begin + 4 * size]
            begin += 4 * size
            outs.append(own.reshape(2, 2, size, own.shape[1]).transpose(2, 0, 1, 3))
        return rows

    for k in range(chunks):
        if k == chunks - 1:
            early = give_back(0, chunks - 3)
        after = [token if k == 0 else send]
        part = right_part(k, *after)
        ((send, keep),) = run(f"right_{k}", 15, after, part)
        sums[k] = send, keep
        if k + 2 < chunks:
            cross(k + 2, send)
    give_back(chunks - 3, chunks - 1, early, send)
    give_back(chunks - 1, chunks)
    return jnp.concatenate(outs, 0)[None]


def solution(mesh):
    return jax.shard_map(
        per_device,
        mesh=mesh,
        in_specs=(
            P("seg", None, None, "row"),
            P("seg", None, None, "row"),
            P("seg", "row"),
            P("seg", None, None, None, None, None),
            P("seg", None, None, "row"),
            P("seg", None, "row", None),
        ),
        out_specs=P("seg", None, None, None, "row"),
        check_vma=False,
    )
```

```python
import jax
import jax.numpy as jnp
from jax import lax
from jax.experimental import pallas as pl
from jax.experimental.pallas import tpu as pltpu
from jax.sharding import PartitionSpec as P

MIB = 1024 * 1024
LANES = 128
WIDE = 256
SLOTS = 4
TOKEN = jax.ShapeDtypeStruct((8, LANES), jnp.float32)
COST = 2 * 10**9
SIZES = (32, 32, 32, 16, 16)
FETCHES = (1, 1, 3)

def shifted(value, axis, steps):
    count = lax.axis_size(axis)
    first, last = (max(0, -steps), min(count, count - steps))
    return lax.ppermute(value, axis, [(source, source + steps) for source in range(first, last)])


def swapped(value, axis, bit):
    count = lax.axis_size(axis)
    return lax.ppermute(value, axis, [(source, source ^ bit) for source in range(count)])


def in_vmem(value):
    return pltpu.with_memory_space_constraint(value, pltpu.VMEM)


def in_hbm(value):
    return pltpu.with_memory_space_constraint(value, pltpu.HBM)


VMEM, SMEM, ANY = (
    pl.BlockSpec(memory_space=space) for space in (pltpu.VMEM, pltpu.SMEM, pl.ANY)
)


def run(name, vmem, after, *parts):
    inputs = [pair for part in parts for pair in part[1]]
    waits = len(after)
    outs = [shape for part in parts for shape in part[2]]
    groups = {id(part[3]): part[3] for part in parts}
    places = dict(zip(groups, [sum(map(len, list(groups.values())[:n])) for n in range(len(groups))]))
    scratch = [shape for group in groups.values() for shape in group]

    def kernel(*refs):
        refs = list(refs)
        ins, refs = refs[:len(inputs)], refs[len(inputs) + waits:]
        results, own = refs[:len(outs)], refs[len(outs):]
        for part in parts:
            taken = []
            for group, number in ((ins, len(part[1])), (results, len(part[2]))):
                taken += group[:number]
                del group[:number]
            place = places[id(part[3])]
            part[0](*taken, *own[place:place + len(part[3])])

    values = pl.pallas_call(
        kernel,
        in_specs=[spec for spec, _ in inputs] + [ANY] * waits,
        out_specs=[VMEM] * len(outs),
        out_shape=outs,
        scratch_shapes=scratch,
        compiler_params=pltpu.CompilerParams(vmem_limit_bytes=vmem * MIB),
        cost_estimate=pl.CostEstimate(flops=COST, bytes_accessed=0, transcendentals=0),
        name=name,
    )(*[value for _, value in inputs], *after)
    values = list(values)
    result = []
    for part in parts:
        result.append(values[:len(part[2])])
        del values[:len(part[2])]
    return result

def halves(x):
    hi = x.astype(jnp.bfloat16)
    lo = (x - hi.astype(jnp.float32)).astype(jnp.bfloat16)
    return hi, lo


def product(both, w_hi, w_lo):
    rows = both.shape[0] // 2
    wide = jnp.dot(both, w_hi, preferred_element_type=jnp.float32)
    return wide[:rows] + wide[rows:] + jnp.dot(
        both[:rows], w_lo, preferred_element_type=jnp.float32
    )


def streamed(x_hbm, buffers, sems, body):
    slots, block = buffers.shape[:2]
    steps = x_hbm.shape[0] // block

    def copy(t):
        slot = lax.rem(t, slots)
        rows = pl.ds(pl.multiple_of(t * block, block), block)
        return pltpu.make_async_copy(x_hbm.at[rows], buffers.at[slot], sems.at[slot])

    for t in range(slots - 1):
        copy(t).start()

    @pl.loop(0, steps)
    def _(t):
        @pl.when(t + slots - 1 < steps)
        def _():
            copy(t + slots - 1).start()

        copy(t).wait()
        body(t, buffers.at[lax.rem(t, slots)])


def split_core(core):
    bond, spins, cols = core.shape
    tiles = cols // LANES
    step = spins * tiles
    block = bond // 8
    flat = core.reshape(bond, spins, tiles, LANES).transpose(0, 2, 1, 3).reshape(bond * step, LANES)

    def body(x_hbm, hi_ref, lo_ref, token_ref, buffers, sems):
        def split(t, x_ref):
            rows = pl.ds(pl.multiple_of(t * block, block), block)
            for tile in range(tiles):
                lanes = slice(tile * LANES, (tile + 1) * LANES)
                for i in range(spins):
                    x = x_ref[pl.ds(tile * spins + i, block, stride=step), :]
                    hi_ref[i, rows, lanes], lo_ref[i, rows, lanes] = halves(x)

        streamed(x_hbm, buffers, sems, split)
        token_ref[...] = jnp.zeros_like(token_ref)

    out = pltpu.VMEM((spins, bond, cols), jnp.bfloat16)
    scratch = [
        pltpu.VMEM((SLOTS, block * step, LANES), jnp.float32),
        pltpu.SemaphoreType.DMA((SLOTS,)),
    ]
    return body, [(ANY, in_hbm(flat))], [out, out, TOKEN], scratch


def split_env(env):
    rows, cols = env.shape
    block = LANES

    def body(x_hbm, hi_ref, lo_ref, token_ref, buffers, sems):
        def split(t, x_ref):
            at = pl.ds(pl.multiple_of(t * block, block), block)
            hi_ref[at, :], lo_ref[at, :] = halves(x_ref[...])

        streamed(x_hbm, buffers, sems, split)
        token_ref[...] = jnp.zeros_like(token_ref)

    out = pltpu.VMEM((rows, cols), jnp.bfloat16)
    scratch = [
        pltpu.VMEM((SLOTS - 1, block, cols), jnp.float32),
        pltpu.SemaphoreType.DMA((SLOTS - 1,)),
    ]
    return body, [(ANY, in_hbm(env))], [out, out, TOKEN], scratch


def cut(env, start, size):
    width, _, cols = env.shape

    def body(env_hbm, out_ref, sem):
        copy = pltpu.make_async_copy(env_hbm.at[:, pl.ds(start, size), :], out_ref, sem)
        copy.start()
        copy.wait()

    out = pltpu.VMEM((width, size, cols), env.dtype)
    return body, [(ANY, in_hbm(env))], [out], [pltpu.SemaphoreType.DMA(())]


def copied(x):
    def body(x_ref, out_ref):
        out_ref[...] = x_ref[...]

    return body, [(VMEM, x)], [jax.ShapeDtypeStruct(x.shape, x.dtype)], []


def added(*pairs):
    rows = [x.shape[0] for x, _ in pairs]

    def body(*refs):
        for n in range(len(pairs)):
            at = slice(sum(rows[:n]), sum(rows[:n + 1]))
            refs[-1][at, :] = refs[2 * n][...] + refs[2 * n + 1][...]

    x = pairs[0][0]
    out = jax.ShapeDtypeStruct((sum(rows), x.shape[1]), x.dtype)
    return body, [(VMEM, value) for pair in pairs for value in pair], [out], []


def summed(x, y):
    def body(x_ref, y_ref, *out_refs):
        for m, out_ref in enumerate(out_refs):
            out_ref[...] = x_ref[m] + y_ref[m]

    outs = [jax.ShapeDtypeStruct(x.shape[1:], x.dtype)] * x.shape[0]
    return body, [(VMEM, x), (VMEM, y)], outs, []


def lay_out(row, pieces, both_ref):
    rows = both_ref.shape[0] // 2
    for d, x in enumerate(pieces):
        cols = x.shape[-1]
        hi, lo = halves(x.reshape(rows, cols))
        at = pl.ds(pl.multiple_of((row ^ d) * cols, cols), cols)
        both_ref[:rows, at] = hi
        both_ref[rows:, at] = lo


def left(row, mpo, pieces, start, panel, core_hi, core_lo, inv):
    width, _, cols = pieces[0].shape
    spins, bond, _ = core_hi.shape
    count = len(pieces)
    wide = min(WIDE, cols)

    def body(row_ref, mpo_ref, *refs):
        pieces = refs[:count]
        hi_ref, lo_ref, inv_ref, out_ref, both_ref, acc_ref = refs[count:]
        lay_out(row_ref[0], [ref[:, start:start + panel, :] for ref in pieces], both_ref)

        @pl.loop(0, spins * (cols // wide))
        def _(n):
            i, at = n % spins, pl.ds(pl.multiple_of(n // spins * wide, wide), wide)
            acc_ref[i, :, at] = product(both_ref[...], hi_ref[i, :, at], lo_ref[i, :, at])

        for c in range(0, cols, wide):
            at = slice(c, c + wide)
            inv = inv_ref[:, at]
            for p in range(2):
                for y in range(width):
                    total = None
                    for w in range(width):
                        for i in range(spins):
                            scalar = mpo_ref[((w * width + y) * 2 + p) * 2 + i]
                            value = scalar * acc_ref[i, w * panel:(w + 1) * panel, at]
                            total = value if total is None else total + value
                    out_ref[p * width + y, :, at] = total * inv

    inputs = [(SMEM, row), (SMEM, mpo)] + [(VMEM, piece) for piece in pieces]
    inputs += [(VMEM, in_vmem(core_hi)), (VMEM, in_vmem(core_lo)), (VMEM, inv)]
    out = jax.ShapeDtypeStruct((2 * width, panel, cols), jnp.float32)
    scratch = [
        pltpu.VMEM((2 * width * panel, bond), jnp.bfloat16),
        pltpu.VMEM((spins, width * panel, cols), jnp.float32),
    ]
    return body, inputs, [out], scratch


def right(row, mpo, pieces, core_hi, core_lo, env_hi, env_lo):
    blocks, panel, cols = pieces[0].shape
    width = blocks // 2
    spins, bond, _ = core_hi.shape
    inner, outer = env_hi.shape
    count = len(pieces)
    half = count // 2
    out_cols = outer // count

    def body(row_ref, mpo_ref, *refs):
        pieces = refs[:count]
        core_hi, core_lo, env_hi, env_lo, send_ref, keep_ref = refs[count:count + 6]
        both_ref, first_ref, mixed_ref = refs[count + 6:]
        row = row_ref[0]
        lay_out(row, [ref[...] for ref in pieces], both_ref)
        wide = min(WIDE, cols)

        for c in range(0, cols, wide):
            at = slice(c, c + wide)
            for j in range(spins):
                first_ref[j, :, at] = product(
                    both_ref[...], core_hi[j, :, at], core_lo[j, :, at]
                )
        for c in range(0, cols, wide):
            at = slice(c, c + wide)
            for p in range(2):
                for q in range(2):
                    to = (p * 2 + q) * panel
                    for z in range(width):
                        total = None
                        for y in range(width):
                            for j in range(spins):
                                scalar = mpo_ref[((y * width + z) * 2 + q) * 2 + j]
                                start = (p * width + y) * panel
                                value = scalar * first_ref[j, start:start + panel, at]
                                total = value if total is None else total + value
                        hi, lo = halves(total)
                        lanes = slice(z * cols + c, z * cols + c + wide)
                        mixed_ref[to:to + panel, lanes] = hi
                        mixed_ref[4 * panel + to:5 * panel + to, lanes] = lo
        narrow = min(WIDE, out_cols)
        for d in [*range(1, count, 2), *range(0, count, 2)]:
            out_ref = send_ref if d % 2 else keep_ref
            for c in range(0, out_cols, narrow):
                at = pl.ds(pl.multiple_of((row ^ d) * out_cols + c, narrow), narrow)
                out_ref[d // 2, :, c:c + narrow] = product(
                    mixed_ref[...], env_hi[:, at], env_lo[:, at]
                )

    inputs = [(SMEM, row), (SMEM, mpo)] + [(VMEM, piece) for piece in pieces]
    inputs += [(VMEM, in_vmem(value)) for value in (core_hi, core_lo, env_hi, env_lo)]
    out = jax.ShapeDtypeStruct((half, 4 * panel, out_cols), jnp.float32)
    scratch = [
        pltpu.VMEM((2 * blocks * panel, bond), jnp.bfloat16),
        pltpu.VMEM((spins, blocks * panel, cols), jnp.float32),
        pltpu.VMEM((8 * panel, inner), jnp.bfloat16),
    ]
    return body, inputs, [out, out], scratch


def reduced(send, keep, axis):
    came = swapped(send, axis, 1)
    if keep.shape[0] == 1:
        return keep[0], came[0]
    (values,) = run("summed", 4, [], summed(keep, came))
    bit = 2
    while True:
        came = [swapped(value, axis, bit) for value in values[1::2]]
        pairs = list(zip(values[0::2], came))
        if len(pairs) == 1:
            return pairs[0]
        values = [value for (value,) in run("added", 4, [], *[added(pair) for pair in pairs])]
        bit *= 2


def per_device(left_env, left_core, inv_sing, mpo_pair, right_core, right_env):
    count = lax.axis_size("row")
    row = lax.axis_index("row").astype(jnp.int32).reshape(1)
    env = left_env[0].transpose(1, 0, 2)
    mpo_left = mpo_pair[0, 0].reshape(-1)
    mpo_sent = mpo_pair[0, 1].reshape(-1)
    mpo_right = shifted(mpo_sent, "seg", 1)
    flat_env = right_env[0].reshape(-1, right_env.shape[3])
    chunks = len(SIZES)

    begins = [sum(SIZES[:k]) for k in range(chunks)]
    firsts = [sum(FETCHES[:f]) for f in range(len(FETCHES))]
    fetched, spread = {}, {}

    def gathered(own, other, *after):
        if after:
            ((other,),) = run("copied", 4, after, copied(other))
        pieces = {0: own, count // 2: other}
        bit = count // 4
        while bit:
            for d in list(pieces):
                pieces[d ^ bit] = swapped(pieces[d], "row", bit)
            bit //= 2
        return [pieces[d] for d in range(count)]

    def fetch(f, *after):
        k, number = firsts[f], FETCHES[f]
        ((own,),) = run("cut", 2, after, cut(env, begins[k], sum(SIZES[k:k + number])))
        fetched[f] = own, swapped(own, "row", count // 2)

    def left_part(k, *after):
        f = max(f for f in range(len(FETCHES)) if firsts[f] <= k)
        if f not in spread:
            spread[f] = gathered(*fetched[f], *after)
        return left(
            row, mpo_left, spread[f], begins[k] - begins[firsts[f]], SIZES[k], *core_a, inv_sing
        )

    fetch(0)
    (((*core_a, token)),) = run("split_a", 10, [row, mpo_left, mpo_sent], split_core(left_core[0]))
    fetch(1, fetched[0][1], token)
    ((scaled,),) = run("left_0", 10, [], left_part(0, token))
    sent, crossed, sums = {}, {}, {}

    def send_on(k, value):
        sent[k] = shifted(value, "seg", 1)

    def cross(k, *after):
        if after:
            ((sent[k],),) = run("copied", 4, after, copied(sent[k]))
        crossed[k] = swapped(sent[k], "row", count // 2)

    def right_part(k, *after):
        return right(row, mpo_right, gathered(sent[k], crossed[k], *after), *core_b, *env_b)

    send_on(0, scaled)
    fetch(2, fetched[1][1], scaled)
    part = left_part(1)
    (scaled,), (*core_b, token) = run("left_1", 14, [scaled], part, split_core(right_core[0]))
    send_on(1, scaled)
    cross(0)
    after = [scaled, token, sent[0], fetched[2][1]]
    parts = [left_part(k, scaled, mpo_right) for k in range(2, chunks)]
    scratches = {part[3][0].shape: part[3] for part in parts}
    parts = [part[:3] + (scratches[part[3][0].shape],) for part in parts]
    (*env_b, token), *rest = run("left_2", 13, after, split_env(flat_env), *parts)
    for k, (scaled,) in enumerate(rest, 2):
        send_on(k, scaled)
    cross(1, token)
    outs = []

    def give_back(first, last, *after):
        pairs = [reduced(*sums[k], "row") for k in range(first, last)]
        ((rows,),) = run("added", 4, after, added(*pairs))
        rows = shifted(rows, "seg", -1)
        begin = 0
        for size in SIZES[first:last]:
            own = rows[begin:begin + 4 * size]
            begin += 4 * size
            outs.append(own.reshape(2, 2, size, own.shape[1]).transpose(2, 0, 1, 3))
        return rows

    for k in range(chunks):
        if k == chunks - 1:
            early = give_back(0, chunks - 3)
        after = [token if k == 0 else send]
        part = right_part(k, *after)
        ((send, keep),) = run(f"right_{k}", 15, after, part)
        sums[k] = send, keep
        if k + 2 < chunks:
            cross(k + 2, send)
    give_back(chunks - 3, chunks - 1, early, send)
    give_back(chunks - 1, chunks)
    return jnp.concatenate(outs, 0)[None]


def solution(mesh):
    return jax.shard_map(
        per_device,
        mesh=mesh,
        in_specs=(
            P("seg", None, None, "row"),
            P("seg", None, None, "row"),
            P("seg", "row"),
            P("seg", None, None, None, None, None),
            P("seg", None, None, "row"),
            P("seg", None, "row", None),
        ),
        out_specs=P("seg", None, None, None, "row"),
        check_vma=False,
    )
```

```python
import jax
import jax.numpy as jnp
from jax import lax
from jax.experimental import pallas as pl
from jax.experimental.pallas import tpu as pltpu
from jax.sharding import PartitionSpec as P

MIB = 1024 * 1024
LANES = 128
WIDE = 256
SLOTS = 4
TOKEN = jax.ShapeDtypeStruct((8, LANES), jnp.float32)
COST = 2 * 10**9
SIZES = (32, 32, 32, 32)
FETCHES = (1, 1, 2)

def shifted(value, axis, steps):
    count = lax.axis_size(axis)
    first, last = (max(0, -steps), min(count, count - steps))
    return lax.ppermute(value, axis, [(source, source + steps) for source in range(first, last)])


def swapped(value, axis, bit):
    count = lax.axis_size(axis)
    return lax.ppermute(value, axis, [(source, source ^ bit) for source in range(count)])


def in_vmem(value):
    return pltpu.with_memory_space_constraint(value, pltpu.VMEM)


def in_hbm(value):
    return pltpu.with_memory_space_constraint(value, pltpu.HBM)


VMEM, SMEM, ANY = (
    pl.BlockSpec(memory_space=space) for space in (pltpu.VMEM, pltpu.SMEM, pl.ANY)
)


def run(name, vmem, after, *parts):
    inputs = [pair for part in parts for pair in part[1]]
    waits = len(after)
    outs = [shape for part in parts for shape in part[2]]
    groups = {id(part[3]): part[3] for part in parts}
    places = dict(zip(groups, [sum(map(len, list(groups.values())[:n])) for n in range(len(groups))]))
    scratch = [shape for group in groups.values() for shape in group]

    def kernel(*refs):
        refs = list(refs)
        ins, refs = refs[:len(inputs)], refs[len(inputs) + waits:]
        results, own = refs[:len(outs)], refs[len(outs):]
        for part in parts:
            taken = []
            for group, number in ((ins, len(part[1])), (results, len(part[2]))):
                taken += group[:number]
                del group[:number]
            place = places[id(part[3])]
            part[0](*taken, *own[place:place + len(part[3])])

    values = pl.pallas_call(
        kernel,
        in_specs=[spec for spec, _ in inputs] + [ANY] * waits,
        out_specs=[VMEM] * len(outs),
        out_shape=outs,
        scratch_shapes=scratch,
        compiler_params=pltpu.CompilerParams(vmem_limit_bytes=vmem * MIB),
        cost_estimate=pl.CostEstimate(
            flops=COST if vmem > 4 else 10**6, bytes_accessed=0, transcendentals=0
        ),
        name=name,
    )(*[value for _, value in inputs], *after)
    values = list(values)
    result = []
    for part in parts:
        result.append(values[:len(part[2])])
        del values[:len(part[2])]
    return result

def halves(x):
    hi = x.astype(jnp.bfloat16)
    lo = (x - hi.astype(jnp.float32)).astype(jnp.bfloat16)
    return hi, lo


def product(both, w_hi, w_lo):
    rows = both.shape[0] // 2
    wide = jnp.dot(both, w_hi, preferred_element_type=jnp.float32)
    return wide[:rows] + wide[rows:] + jnp.dot(
        both[:rows], w_lo, preferred_element_type=jnp.float32
    )


def streamed(x_hbm, buffers, sems, body):
    slots, block = buffers.shape[:2]
    steps = x_hbm.shape[0] // block

    def copy(t):
        slot = lax.rem(t, slots)
        rows = pl.ds(pl.multiple_of(t * block, block), block)
        return pltpu.make_async_copy(x_hbm.at[rows], buffers.at[slot], sems.at[slot])

    for t in range(slots - 1):
        copy(t).start()

    @pl.loop(0, steps)
    def _(t):
        @pl.when(t + slots - 1 < steps)
        def _():
            copy(t + slots - 1).start()

        copy(t).wait()
        body(t, buffers.at[lax.rem(t, slots)])


def split_core(core):
    bond, spins, cols = core.shape
    tiles = cols // LANES
    step = spins * tiles
    block = bond // 8
    flat = core.reshape(bond, spins, tiles, LANES).transpose(0, 2, 1, 3).reshape(bond * step, LANES)

    def body(x_hbm, hi_ref, lo_ref, token_ref, buffers, sems):
        def split(t, x_ref):
            rows = pl.ds(pl.multiple_of(t * block, block), block)
            for tile in range(tiles):
                lanes = slice(tile * LANES, (tile + 1) * LANES)
                for i in range(spins):
                    x = x_ref[pl.ds(tile * spins + i, block, stride=step), :]
                    hi_ref[i, rows, lanes], lo_ref[i, rows, lanes] = halves(x)

        streamed(x_hbm, buffers, sems, split)
        token_ref[...] = jnp.zeros_like(token_ref)

    out = pltpu.VMEM((spins, bond, cols), jnp.bfloat16)
    scratch = [
        pltpu.VMEM((SLOTS, block * step, LANES), jnp.float32),
        pltpu.SemaphoreType.DMA((SLOTS,)),
    ]
    return body, [(ANY, in_hbm(flat))], [out, out, TOKEN], scratch


def split_env(env):
    rows, cols = env.shape
    block = LANES

    def body(x_hbm, hi_ref, lo_ref, token_ref, buffers, sems):
        def split(t, x_ref):
            at = pl.ds(pl.multiple_of(t * block, block), block)
            hi_ref[at, :], lo_ref[at, :] = halves(x_ref[...])

        streamed(x_hbm, buffers, sems, split)
        token_ref[...] = jnp.zeros_like(token_ref)

    out = pltpu.VMEM((rows, cols), jnp.bfloat16)
    scratch = [
        pltpu.VMEM((SLOTS, block, cols), jnp.float32),
        pltpu.SemaphoreType.DMA((SLOTS,)),
    ]
    return body, [(ANY, in_hbm(env))], [out, out, TOKEN], scratch


def cut(env, start, size):
    width, _, cols = env.shape

    def body(env_hbm, out_ref, sem):
        copy = pltpu.make_async_copy(env_hbm.at[:, pl.ds(start, size), :], out_ref, sem)
        copy.start()
        copy.wait()

    out = pltpu.VMEM((width, size, cols), env.dtype)
    return body, [(ANY, in_hbm(env))], [out], [pltpu.SemaphoreType.DMA(())]


def copied(x):
    def body(x_ref, out_ref):
        out_ref[...] = x_ref[...]

    return body, [(VMEM, x)], [jax.ShapeDtypeStruct(x.shape, x.dtype)], []


def added(*pairs):
    rows = [x.shape[0] for x, _ in pairs]

    def body(*refs):
        for n in range(len(pairs)):
            at = slice(sum(rows[:n]), sum(rows[:n + 1]))
            refs[-1][at, :] = refs[2 * n][...] + refs[2 * n + 1][...]

    x = pairs[0][0]
    out = jax.ShapeDtypeStruct((sum(rows), x.shape[1]), x.dtype)
    return body, [(VMEM, value) for pair in pairs for value in pair], [out], []


def summed(x, y):
    def body(x_ref, y_ref, *out_refs):
        for m, out_ref in enumerate(out_refs):
            out_ref[...] = x_ref[m] + y_ref[m]

    outs = [jax.ShapeDtypeStruct(x.shape[1:], x.dtype)] * x.shape[0]
    return body, [(VMEM, x), (VMEM, y)], outs, []


def lay_out(row, pieces, both_ref):
    rows = both_ref.shape[0] // 2
    for d, x in enumerate(pieces):
        cols = x.shape[-1]
        hi, lo = halves(x.reshape(rows, cols))
        at = pl.ds(pl.multiple_of((row ^ d) * cols, cols), cols)
        both_ref[:rows, at] = hi
        both_ref[rows:, at] = lo


def left(row, mpo, pieces, start, panel, core_hi, core_lo, inv):
    width, _, cols = pieces[0].shape
    spins, bond, _ = core_hi.shape
    count = len(pieces)
    wide = min(WIDE, cols)

    def body(row_ref, mpo_ref, *refs):
        pieces = refs[:count]
        hi_ref, lo_ref, inv_ref, out_ref, both_ref, acc_ref = refs[count:]
        lay_out(row_ref[0], [ref[:, start:start + panel, :] for ref in pieces], both_ref)

        @pl.loop(0, spins * (cols // wide))
        def _(n):
            i, at = n % spins, pl.ds(pl.multiple_of(n // spins * wide, wide), wide)
            acc_ref[i, :, at] = product(both_ref[...], hi_ref[i, :, at], lo_ref[i, :, at])

        for c in range(0, cols, wide):
            at = slice(c, c + wide)
            inv = inv_ref[:, at]
            for p in range(2):
                for y in range(width):
                    total = None
                    for w in range(width):
                        for i in range(spins):
                            scalar = mpo_ref[((w * width + y) * 2 + p) * 2 + i]
                            value = scalar * acc_ref[i, w * panel:(w + 1) * panel, at]
                            total = value if total is None else total + value
                    out_ref[p * width + y, :, at] = total * inv

    inputs = [(SMEM, row), (SMEM, mpo)] + [(VMEM, piece) for piece in pieces]
    inputs += [(VMEM, in_vmem(core_hi)), (VMEM, in_vmem(core_lo)), (VMEM, inv)]
    out = jax.ShapeDtypeStruct((2 * width, panel, cols), jnp.float32)
    scratch = [
        pltpu.VMEM((2 * width * panel, bond), jnp.bfloat16),
        pltpu.VMEM((spins, width * panel, cols), jnp.float32),
    ]
    return body, inputs, [out], scratch


def right(row, mpo, pieces, core_hi, core_lo, env_hi, env_lo):
    blocks, panel, cols = pieces[0].shape
    width = blocks // 2
    spins, bond, _ = core_hi.shape
    inner, outer = env_hi.shape
    count = len(pieces)
    half = count // 2
    out_cols = outer // count

    def body(row_ref, mpo_ref, *refs):
        pieces = refs[:count]
        core_hi, core_lo, env_hi, env_lo, send_ref, keep_ref = refs[count:count + 6]
        both_ref, first_ref, mixed_ref = refs[count + 6:]
        row = row_ref[0]
        lay_out(row, [ref[...] for ref in pieces], both_ref)
        wide = min(WIDE, cols)

        @pl.loop(0, spins * (cols // wide))
        def _(n):
            j, at = n % spins, pl.ds(pl.multiple_of(n // spins * wide, wide), wide)
            first_ref[j, :, at] = product(both_ref[...], core_hi[j, :, at], core_lo[j, :, at])

        for c in range(0, cols, wide):
            at = slice(c, c + wide)
            for p in range(2):
                for q in range(2):
                    to = (p * 2 + q) * panel
                    for z in range(width):
                        total = None
                        for y in range(width):
                            for j in range(spins):
                                scalar = mpo_ref[((y * width + z) * 2 + q) * 2 + j]
                                start = (p * width + y) * panel
                                value = scalar * first_ref[j, start:start + panel, at]
                                total = value if total is None else total + value
                        hi, lo = halves(total)
                        lanes = slice(z * cols + c, z * cols + c + wide)
                        mixed_ref[to:to + panel, lanes] = hi
                        mixed_ref[4 * panel + to:5 * panel + to, lanes] = lo
        narrow = min(WIDE, out_cols)
        for parity, out_ref in ((1, send_ref), (0, keep_ref)):

            @pl.loop(0, half * (out_cols // narrow))
            def _(n):
                m, c = n % half, pl.multiple_of(n // half * narrow, narrow)
                source = pl.multiple_of((row ^ (2 * m + parity)) * out_cols + c, narrow)
                at = pl.ds(source, narrow)
                out_ref[m, :, pl.ds(c, narrow)] = product(
                    mixed_ref[...], env_hi[:, at], env_lo[:, at]
                )

    inputs = [(SMEM, row), (SMEM, mpo)] + [(VMEM, piece) for piece in pieces]
    inputs += [(VMEM, in_vmem(value)) for value in (core_hi, core_lo, env_hi, env_lo)]
    out = jax.ShapeDtypeStruct((half, 4 * panel, out_cols), jnp.float32)
    scratch = [
        pltpu.VMEM((2 * blocks * panel, bond), jnp.bfloat16),
        pltpu.VMEM((spins, blocks * panel, cols), jnp.float32),
        pltpu.VMEM((8 * panel, inner), jnp.bfloat16),
    ]
    return body, inputs, [out, out], scratch


def halved(send, keep, axis):
    came = swapped(send, axis, 1)
    if keep.shape[0] == 1:
        return [(keep[0], came[0])]
    return run("summed", 4, [], summed(keep, came))[0]


def reduced(values, axis):
    if len(values) == 1:
        return values[0]
    bit = 2
    while True:
        came = [swapped(value, axis, bit) for value in values[1::2]]
        pairs = list(zip(values[0::2], came))
        if len(pairs) == 1:
            return pairs[0]
        values = [value for (value,) in run("added", 4, [], *[added(pair) for pair in pairs])]
        bit *= 2


def per_device(left_env, left_core, inv_sing, mpo_pair, right_core, right_env):
    count = lax.axis_size("row")
    row = lax.axis_index("row").astype(jnp.int32).reshape(1)
    env = left_env[0].transpose(1, 0, 2)
    mpo_left = mpo_pair[0, 0].reshape(-1)
    mpo_sent = mpo_pair[0, 1].reshape(-1)
    mpo_right = shifted(mpo_sent, "seg", 1)
    flat_env = right_env[0].reshape(-1, right_env.shape[3])
    chunks = len(SIZES)

    begins = [sum(SIZES[:k]) for k in range(chunks)]
    firsts = [sum(FETCHES[:f]) for f in range(len(FETCHES))]
    fetched, spread = {}, {}

    def gathered(own, other, *after):
        if after:
            ((other,),) = run("copied", 4, after, copied(other))
        pieces = {0: own, count // 2: other}
        bit = count // 4
        while bit:
            for d in list(pieces):
                pieces[d ^ bit] = swapped(pieces[d], "row", bit)
            bit //= 2
        return [pieces[d] for d in range(count)]

    def fetch(f, *after):
        k, number = firsts[f], FETCHES[f]
        ((own,),) = run("cut", 2, after, cut(env, begins[k], sum(SIZES[k:k + number])))
        fetched[f] = own, swapped(own, "row", count // 2)

    def left_part(k, *after):
        f = max(f for f in range(len(FETCHES)) if firsts[f] <= k)
        if f not in spread:
            spread[f] = gathered(*fetched[f], *after)
        return left(
            row, mpo_left, spread[f], begins[k] - begins[firsts[f]], SIZES[k], *core_a, inv_sing
        )

    fetch(0)
    fetch(1, fetched[0][0])
    fetch(2, fetched[1][0])
    (((*core_a, token)),) = run("split_a", 10, [row, mpo_left, mpo_sent, fetched[2][0]], split_core(left_core[0]))
    ((scaled,),) = run("left_0", 10, [], left_part(0, token))
    sent, crossed, sums = {}, {}, {}

    def send_on(k, value):
        sent[k] = shifted(value, "seg", 1)

    def cross(k, *after):
        if after:
            ((sent[k],),) = run("copied", 4, after, copied(sent[k]))
        crossed[k] = swapped(sent[k], "row", count // 2)

    def right_part(k, *after):
        return right(row, mpo_right, gathered(sent[k], crossed[k], *after), *core_b, *env_b)

    send_on(0, scaled)
    part = left_part(1)
    (scaled,), (*core_b, token) = run("left_1", 14, [scaled], part, split_core(right_core[0]))
    send_on(1, scaled)
    cross(0)
    after = [scaled, token, sent[0], fetched[2][1]]
    parts = [left_part(k, scaled, mpo_right) for k in range(2, chunks)]
    scratches = {part[3][0].shape: part[3] for part in parts}
    parts = [part[:3] + (scratches[part[3][0].shape],) for part in parts]
    (*env_b, token), *rest = run("left_2", 13, after, split_env(flat_env), *parts)
    for k, (scaled,) in enumerate(rest, 2):
        send_on(k, scaled)
    cross(1, token)
    outs = []

    def give_back(first, last, *after):
        pairs = [reduced(sums[k], "row") for k in range(first, last)]
        ((rows,),) = run("added", 4, after, added(*pairs))
        rows = shifted(rows, "seg", -1)
        begin = 0
        for size in SIZES[first:last]:
            own = rows[begin:begin + 4 * size]
            begin += 4 * size
            outs.append(own.reshape(2, 2, size, own.shape[1]).transpose(2, 0, 1, 3))
        return rows

    for k in range(chunks):
        if k == chunks - 1:
            early = give_back(0, chunks - 3)
        after = [token if k == 0 else send]
        part = right_part(k, *after)
        if k >= 2:
            after += sums[k - 2][-1:]
        ((send, keep),) = run(f"right_{k}", 15, after, part)
        sums[k] = halved(send, keep, "row")
        if k + 2 < chunks:
            cross(k + 2, send)
    give_back(chunks - 3, chunks - 1, early, send)
    give_back(chunks - 1, chunks)
    return jnp.concatenate(outs, 0)[None]


def solution(mesh):
    return jax.shard_map(
        per_device,
        mesh=mesh,
        in_specs=(
            P("seg", None, None, "row"),
            P("seg", None, None, "row"),
            P("seg", "row"),
            P("seg", None, None, None, None, None),
            P("seg", None, None, "row"),
            P("seg", None, "row", None),
        ),
        out_specs=P("seg", None, None, None, "row"),
        check_vma=False,
    )
```
